32 devices in a mesh: chan: 8 (over y, x, core), win: 4 (over z).
Axes of the slice: x: 2, y: 2, z: 4, core: 2. Of those that a mesh axis runs over, the one named last changes fastest.
Arguments:
- strain: bfloat16 [384, 4, 1024], P('chan', 'win'), may hold values from -384 to 384
- seg_ids: int32 [384], replicated, may hold values from 0 to 31, never falling along the last dimension, each value on 1 to 24 neighbouring positions
- dead: int32 [32], replicated, may hold values 0 or 1
- radius: int32 [384], P('chan'), may hold values from 1 to 8, as said below
Outputs:
- cross_spectra: bfloat16 [4, 2, 384, 384], P('win', None, 'chan')
The draws below stay inside these ranges and needn't reach their ends.
Inputs may be any that keep to these rules, and one draw needn't show every extreme that they name: `seg_ids`: segment numbers never fall along the fiber; a change of segment between neighbouring channels marks a splice. Every segment has 1 to 24 channels, and one has exactly that many. Some channel has radius 8.
All inputs are finite; a program needn't handle non-finite values.
Results may differ from the reference program's by a relative error of at most 0.0023.
Values may be sent and summed in bfloat16 or wider, within the bound.
A program may use at most 64 MiB of HBM per device.

```python
import math
import jax
import jax.numpy as jnp
import numpy as np
from jax import lax

CHAN_DEV = 48
SAMPLES = 1024
FREQ_BINS = 128
FIRST_BIN = 8
SMOOTH_BINS = 4
MOST_REACH = 8
SEG_DEV = 4
CHANNELS = 384
WINDOWS = 4
SEGMENTS = 32
BANDS = 4
BAND_BINS = 32


def draw_strain(key, part):
    keys = jax.random.split(key, 3)
    chan_scale = jnp.exp(jax.random.uniform(keys[0], (CHANNELS, 1, 1), minval=math.log(0.25), maxval=math.log(2.5)))
    window_scale = jnp.exp(jax.random.uniform(keys[1], (CHANNELS, WINDOWS, 1), minval=math.log(0.5), maxval=math.log(2.0)))
    noise = jax.random.truncated_normal(keys[2], -5.0, 5.0, (CHANNELS, WINDOWS, SAMPLES))
    sample_pos = jnp.arange(SAMPLES).astype(jnp.float32)
    edge_taper = 0.5 - 0.5 * jnp.cos(2.0 * math.pi / SAMPLES * (sample_pos + 0.5))
    envelope = 1.0 / jnp.maximum(edge_taper, 1.0 / 16.0)
    values = chan_scale * window_scale * noise * envelope[None, None, :]
    return jnp.clip(values, -384.0, 384.0).astype(jnp.bfloat16)


def draw_radius(key, part):
    spans = jax.random.randint(key, (CHANNELS,), 1, MOST_REACH + 1)
    chosen = jax.random.randint(jax.random.fold_in(key, 7), (), 0, CHANNELS)
    return jnp.where(jnp.arange(CHANNELS) == chosen, MOST_REACH, spans).astype(jnp.int32)


def touch_ends(drawn, rng, smallest, top_value):
    extent = drawn.shape
    index_at = [jax.random.randint(jax.random.fold_in(rng, axis), (), 0, extent[axis]) for axis in range(len(extent))]
    drawn = drawn.at[tuple(index_at)].set(smallest)
    longest = extent.index(max(extent))
    index_at[longest] = (index_at[longest] + 1) % extent[longest]
    return drawn.at[tuple(index_at)].set(top_value)


def length_profile(count, total, bound, skew):
    portions = [(1 << 20) // math.isqrt(grade ** skew) + 1 for grade in range(2, count + 1)]
    spare, given = total - bound - (count - 1), [1] * (count - 1)
    while spare > 0:
        movable = [i for i in range(count - 1) if given[i] < bound]
        pool, budget = sum([portions[i] for i in movable]), spare
        for i in movable:
            extra = min(bound - given[i], max(1, budget * portions[i] // pool), spare)
            given[i] = given[i] + extra
            spare = spare - extra
    return np.array([bound] + given)


def uneven_parts(key, amount, total, most, lean):
    if amount == 2:
        one = jax.random.randint(key, (), max(1, total - most), min(most, total - 1) + 1)
        return jnp.stack([one, total - one])
    sizes = jnp.asarray(length_profile(amount, total, most, lean), jnp.int32)
    twos = (amount - 1) // 2
    source_of, taker = sizes[1:1 + 2 * twos:2], sizes[2:2 + 2 * twos:2]
    margin = jnp.minimum(source_of - 1, most - taker)
    shifted = jax.random.randint(jax.random.fold_in(key, 1), (twos,), 0, 1 << 20) % (margin + 1)
    sizes = sizes.at[1:1 + 2 * twos:2].set(source_of - shifted).at[2:2 + 2 * twos:2].set(taker + shifted)
    return sizes[jax.random.permutation(jax.random.fold_in(key, 2), amount)]


def setup_inputs(seed: int = 0) -> dict:
    streams_of = jax.random.split(jax.random.key(seed), 5)
    return {
        "strain": draw_strain(jax.random.fold_in(streams_of[4], 71), 0),
        "seg_ids": jnp.searchsorted(jnp.cumsum(uneven_parts(streams_of[1], SEGMENTS, CHANNELS, 2 * CHAN_DEV // SEG_DEV, 0)), jnp.arange(CHANNELS), side="right").astype(jnp.int32),
        "dead": touch_ends((jax.random.randint(streams_of[2], (SEGMENTS,), 0, 8) < 1).astype(jnp.int32), jax.random.fold_in(streams_of[2], 1), 0, 1),
        "radius": draw_radius(jax.random.fold_in(streams_of[4], 71), 0),
    }


FLOOR_POWER = 0.01

def fourier_table():
    sample_ids = jnp.arange(SAMPLES, dtype=jnp.int32)
    bin_ids = FIRST_BIN + jnp.arange(FREQ_BINS, dtype=jnp.int32)
    phase_ids = sample_ids[:, None] * bin_ids[None, :] % SAMPLES
    angles = 2.0 * jnp.pi / SAMPLES * phase_ids.astype(jnp.float32)
    taper = 0.5 - 0.5 * jnp.cos(2.0 * jnp.pi / SAMPLES * (sample_ids.astype(jnp.float32) + 0.5))
    weights = taper[:, None] / jnp.sqrt(jnp.float32(SAMPLES))
    return jnp.concatenate([weights * jnp.cos(angles), -weights * jnp.sin(angles)], axis=1)

def smoothing_table():
    bin_ids = jnp.arange(FREQ_BINS, dtype=jnp.int32)
    nearby = (jnp.abs(bin_ids[:, None] - bin_ids[None, :]) <= SMOOTH_BINS).astype(jnp.float32)
    return nearby / lax.optimization_barrier(jnp.sum(nearby, axis=0, keepdims=True))

def swapped_parts(flat, windows):
    parts = flat.reshape(flat.shape[:-1] + (windows, 2, -1))
    turned = jnp.stack([-parts[..., 1, :], parts[..., 0, :]], axis=-2)
    return turned.reshape(flat.shape)

def reference(strain, seg_ids, dead, radius):
    seg_padded = jnp.pad(seg_ids, (MOST_REACH, MOST_REACH), constant_values=-1)
    segment_ids = jnp.arange(SEGMENTS, dtype=jnp.int32)
    dead_padded = lax.optimization_barrier(jnp.sum(jnp.where(seg_padded[:, None] == segment_ids[None, :], dead[None, :], 0), axis=1))
    alive_padded = jnp.where(seg_padded >= 0, 1 - dead_padded, 0)
    strain_wide = strain.astype(jnp.float32)
    padded = jnp.pad(strain_wide, ((MOST_REACH, MOST_REACH), (0, 0), (0, 0)))
    neighbor_sums = jnp.zeros(strain_wide.shape, jnp.float32)
    counts = jnp.zeros((CHANNELS,), jnp.float32)
    for offset in range(-MOST_REACH, MOST_REACH + 1):
        low_row = MOST_REACH + offset
        linked = (seg_padded[low_row:low_row + CHANNELS] == seg_ids) & (alive_padded[low_row:low_row + CHANNELS] > 0) & (abs(offset) <= radius)
        linked_f = linked.astype(jnp.float32)
        neighbor_sums = neighbor_sums + linked_f[:, None, None] * padded[low_row:low_row + CHANNELS]
        counts = counts + linked_f
    counts = jnp.maximum(counts, 1.0)
    alive_own = alive_padded[MOST_REACH:MOST_REACH + CHANNELS].astype(jnp.float32)
    filtered = alive_own[:, None, None] * (strain_wide - neighbor_sums / counts[:, None, None])
    spectra = jnp.dot(filtered.reshape(-1, SAMPLES), fourier_table(), precision=lax.Precision.HIGHEST)
    power_bins = spectra[:, :FREQ_BINS] ** 2 + spectra[:, FREQ_BINS:] ** 2
    smoothed = jnp.dot(power_bins, smoothing_table(), precision=lax.Precision.HIGHEST)
    inverse_amp = lax.rsqrt(jnp.maximum(smoothed, FLOOR_POWER))
    whitened = spectra * jnp.concatenate([inverse_amp, inverse_amp], axis=1)
    banded = whitened.reshape(CHANNELS, WINDOWS, 2, BANDS, BAND_BINS)
    inverse_count = 1.0 / (WINDOWS * BAND_BINS)

    def one_band(band):
        block_band = lax.dynamic_index_in_dim(banded, band, axis=3, keepdims=False).reshape(CHANNELS, -1)
        turned = swapped_parts(block_band, WINDOWS)
        real_part = jnp.dot(block_band, block_band.T, precision=lax.Precision.HIGHEST)
        real_part = (real_part * inverse_count).astype(jnp.bfloat16)
        imag_part = jnp.dot(block_band, turned.T, precision=lax.Precision.HIGHEST)
        imag_part = (imag_part * inverse_count).astype(jnp.bfloat16)
        return jnp.stack([real_part, imag_part], axis=0)
    return lax.map(one_band, jnp.arange(BANDS, dtype=jnp.int32))
```

```python
import functools

import jax
import jax.numpy as jnp
import numpy as np
from jax import lax
from jax.experimental import pallas as pl
from jax.experimental.pallas import tpu as pltpu
from jax.sharding import PartitionSpec as P

SAMPLES = 1024
FREQ_BINS = 128
FIRST_BIN = 8
SMOOTH_BINS = 4
MOST_REACH = 8
FLOOR_POWER = 0.01
LANES = 128
TABLE_CUTS = 4
GROUP = 8

MESH = pl.DeviceIdType.MESH
F32 = jnp.float32
BF16 = jnp.bfloat16


def fourier_table(bands):
    band_bins = FREQ_BINS // bands
    t = np.arange(SAMPLES, dtype=np.int64)
    bins = FIRST_BIN + np.arange(FREQ_BINS, dtype=np.int64)
    angles = 2.0 * np.pi / SAMPLES * (t[:, None] * bins[None, :] % SAMPLES)
    taper = 0.5 - 0.5 * np.cos(2.0 * np.pi / SAMPLES * (t + 0.5))
    weights = taper[:, None] / np.sqrt(float(SAMPLES))
    cos, sin = weights * np.cos(angles), -weights * np.sin(angles)
    both = np.stack(
        [cos.reshape(SAMPLES, bands, band_bins), sin.reshape(SAMPLES, bands, band_bins)], axis=2
    ).reshape(SAMPLES, 2 * FREQ_BINS)
    return both.astype(np.float32).reshape(TABLE_CUTS, SAMPLES // TABLE_CUTS, -1)


def split3(x):
    high = x.astype(BF16)
    rest = x - high.astype(F32)
    middle = rest.astype(BF16)
    low = (rest - middle.astype(F32)).astype(BF16)
    return high, middle, low


def column_of(row, length, shift=0):
    shape = (length, row.shape[1])
    hit = lax.broadcasted_iota(jnp.int32, shape, 1) == lax.broadcasted_iota(jnp.int32, shape, 0) + shift
    return jnp.sum(jnp.where(hit, row, 0), axis=1, keepdims=True)


def links(seg, dead, radius, me, rows):
    channels, segments = seg.shape[1], dead.shape[1]
    start = me * rows - MOST_REACH
    turned = pltpu.roll(jnp.broadcast_to(seg, (8, channels)), lax.rem(channels - start, channels), 1)
    near = turned[0:1, 0:LANES]
    lane = lax.broadcasted_iota(jnp.int32, (1, LANES), 1)
    inside = (lane + start >= 0) & (lane + start < channels)
    dead_column = column_of(dead, segments)
    is_segment = lax.broadcasted_iota(jnp.int32, (segments, LANES), 0) == near
    dead_near = jnp.sum(jnp.where(is_segment, dead_column, 0), axis=0, keepdims=True)
    alive_near = jnp.where(inside, 1 - dead_near, 0)
    own_segs = column_of(near, rows, MOST_REACH)
    alive_own = column_of(alive_near, rows, MOST_REACH).astype(F32)
    reach = column_of(radius, rows)
    shape = (rows, LANES)
    offsets = lax.broadcasted_iota(jnp.int32, shape, 1) - lax.broadcasted_iota(jnp.int32, shape, 0) - MOST_REACH
    linked = (jnp.abs(offsets) <= reach) & (near == own_segs) & (alive_near > 0)
    linked = jnp.where(linked, 1.0, 0.0)
    counts = jnp.maximum(jnp.sum(linked, axis=1, keepdims=True), 1.0)
    return linked[:, : rows + 2 * MOST_REACH].astype(BF16), alive_own, 1.0 / counts


def bin_of(lanes, bands):
    half = FREQ_BINS // bands
    return lanes // (2 * half) * half + lanes % half


def smoothing(bands):
    shape = (2 * FREQ_BINS, 2 * FREQ_BINS)
    apart = bin_of(lax.broadcasted_iota(jnp.int32, shape, 0), bands) - bin_of(
        lax.broadcasted_iota(jnp.int32, shape, 1), bands
    )
    nearby = jnp.where(jnp.abs(apart) <= SMOOTH_BINS, 1.0, 0.0).astype(BF16)
    bins = bin_of(lax.broadcasted_iota(jnp.int32, (1, 2 * FREQ_BINS), 1), bands)
    members = jnp.minimum(bins + SMOOTH_BINS, FREQ_BINS - 1) - jnp.maximum(bins - SMOOTH_BINS, 0) + 1
    return nearby, 1.0 / members.astype(F32)


def dot(a, b):
    return jnp.dot(a, b, preferred_element_type=F32)


def dot_rows(a, b):
    return lax.dot_general(a, b, (((1,), (1,)), ((), ())), preferred_element_type=F32)


def kernel(
    chans, wins, strain_ref, seg_ref, dead_ref, radius_ref, table_hbm, out_ref,
    table, ext, blocks, chunks, table_sem,
    halo_send, halo_recv, win_send, win_recv, own_send, own_recv, rest_send, rest_recv,
):
    rows = strain_ref.shape[0]
    width = 2 * FREQ_BINS
    me, win = lax.axis_index("chan"), lax.axis_index("win")

    loads = [
        pltpu.make_async_copy(table_hbm.at[i], table.at[i], table_sem.at[i]) for i in range(TABLE_CUTS)
    ]
    for load in loads:
        load.start()

    barrier = pltpu.get_barrier_semaphore()

    def greet(k, carry):
        pl.semaphore_signal(barrier, inc=1, device_id={"chan": lax.rem(me + k, chans)}, device_id_type=MESH)
        return carry

    lax.fori_loop(1, chans, greet, 0)
    for r in range(1, wins):
        pl.semaphore_signal(barrier, inc=1, device_id={"win": lax.rem(win + r, wins)}, device_id_type=MESH)

    linked, alive, per_count = links(seg_ref[...], dead_ref[...], radius_ref[...], me, rows)
    nearby, per_member = smoothing(wins)

    total = None
    cut = SAMPLES // TABLE_CUTS
    for i in range(TABLE_CUTS):
        loads[i].wait()
        term = dot(strain_ref[:, i * cut : (i + 1) * cut], jnp.concatenate(split3(table[i]), axis=1))
        total = term if total is None else total + term
    own = total[:, :width] + total[:, width : 2 * width] + total[:, 2 * width :]
    ext[MOST_REACH : MOST_REACH + rows, :] = own

    pl.semaphore_wait(barrier, chans - 1 + wins - 1)

    halos = [
        pltpu.make_async_remote_copy(
            src_ref=ext.at[pl.ds(rows, MOST_REACH)],
            dst_ref=ext.at[pl.ds(0, MOST_REACH)],
            send_sem=halo_send.at[0],
            recv_sem=halo_recv.at[0],
            device_id={"chan": lax.rem(me + 1, chans)},
            device_id_type=MESH,
        ),
        pltpu.make_async_remote_copy(
            src_ref=ext.at[pl.ds(MOST_REACH, MOST_REACH)],
            dst_ref=ext.at[pl.ds(rows + MOST_REACH, MOST_REACH)],
            send_sem=halo_send.at[1],
            recv_sem=halo_recv.at[1],
            device_id={"chan": lax.rem(me + chans - 1, chans)},
            device_id_type=MESH,
        ),
    ]
    for halo in halos:
        halo.start()
    for halo in halos:
        halo.wait_recv()

    sums = dot(linked, jnp.concatenate(split3(ext[...]), axis=1))
    sums = sums[:, :width] + sums[:, width : 2 * width] + sums[:, 2 * width :]
    spectra = alive * (own - sums * per_count)
    smooth = dot(jnp.concatenate(split3(spectra * spectra), axis=0), nearby)
    smooth = (smooth[:rows] + smooth[rows : 2 * rows] + smooth[2 * rows :]) * per_member
    white = spectra * lax.rsqrt(jnp.maximum(smooth, FLOOR_POWER))

    high = white.astype(BF16).astype(F32)
    low = white - high
    part_lanes = width // wins
    for b in range(wins):
        at = slice(b * part_lanes, (b + 1) * part_lanes)
        chunks[b] = jnp.concatenate([high[:, at], low[:, at]], axis=1).astype(BF16)

    to_band = []
    for r in range(1, wins):
        band = lax.rem(win + wins - r, wins)
        copy = pltpu.make_async_remote_copy(
            src_ref=chunks.at[band],
            dst_ref=blocks.at[me, r],
            send_sem=win_send.at[r],
            recv_sem=win_recv.at[r],
            device_id={"win": band},
            device_id_type=MESH,
        )
        copy.start()
        to_band.append(copy)

    blocks[me, 0] = chunks[win]

    def piece(owner, peer, slots, send, recv):
        return pltpu.make_async_remote_copy(
            src_ref=blocks.at[owner, slots],
            dst_ref=blocks.at[owner, slots],
            send_sem=send,
            recv_sem=recv,
            device_id={"chan": peer},
            device_id_type=MESH,
        )

    first, others = pl.ds(0, 1), pl.ds(1, wins - 1)

    def send_first(k, carry):
        piece(me, lax.rem(me + k, chans), first, own_send.at[k], own_recv.at[me]).start()
        return carry

    def send_others(k, carry):
        piece(me, lax.rem(me + k, chans), others, rest_send.at[k], rest_recv.at[me]).start()
        return carry

    lax.fori_loop(1, chans, send_first, 0)
    for copy in to_band:
        copy.wait_recv()
    lax.fori_loop(1, chans, send_others, 0)

    band_bins = part_lanes // 2
    lane = lax.broadcasted_iota(jnp.int32, (rows, 2 * part_lanes), 1)
    is_re = lane % part_lanes < band_bins
    is_high = lane < part_lanes
    left = []
    for r in range(wins):
        block = blocks[me, r].astype(F32)
        swapped = pltpu.roll(block, part_lanes, 1)
        both_high = jnp.where(is_high, block, swapped)
        low_first = jnp.where(is_high, swapped, 0.0)
        sides = []
        for x in (both_high, low_first):
            after = pltpu.roll(x, 2 * part_lanes - band_bins, 1)
            before = pltpu.roll(x, band_bins, 1)
            sides += [x, jnp.where(is_re, after, -before)]
        left.append(jnp.concatenate(sides, axis=0).astype(BF16))

    def wait_piece(k, carry):
        peer = lax.rem(me + k, chans)
        piece(peer, peer, first, own_send.at[k], own_recv.at[peer]).wait_recv()
        piece(peer, peer, others, rest_send.at[k], rest_recv.at[peer]).wait_recv()
        return carry

    lax.fori_loop(1, chans, wait_piece, 0)

    scale = 1.0 / FREQ_BINS

    def product(g):
        acc = None
        for r in range(0, wins, 2):
            right = jnp.concatenate(
                [blocks[pl.ds(g * GROUP, GROUP), r + j].reshape(GROUP * rows, LANES) for j in range(2)], axis=1
            )
            term = dot_rows(jnp.concatenate(left[r : r + 2], axis=1), right)
            acc = term if acc is None else acc + term
        return ((acc[: 2 * rows] + acc[2 * rows :]) * scale).astype(out_ref.dtype)

    if chans == GROUP:
        out = product(0)
        out_ref[0, 0] = out[:rows]
        out_ref[0, 1] = out[rows:]
    else:

        @pl.loop(0, chans // GROUP)
        def _(g):
            out = product(g)
            at = pl.ds(pl.multiple_of(g * (GROUP * rows), LANES), GROUP * rows)
            out_ref[0, 0, :, at] = out[:rows]
            out_ref[0, 1, :, at] = out[rows:]

    for copy in halos + to_band:
        copy.wait_send()

    def wait_sent(k, carry):
        peer = lax.rem(me + k, chans)
        piece(me, peer, first, own_send.at[k], own_recv.at[me]).wait_send()
        piece(me, peer, others, rest_send.at[k], rest_recv.at[me]).wait_send()
        return carry

    lax.fori_loop(1, chans, wait_sent, 0)


def body(chans, wins, strain, seg_ids, dead, radius):
    rows, windows, samples = strain.shape
    table = jnp.asarray(fourier_table(wins))
    width = 2 * FREQ_BINS
    dma = pltpu.SemaphoreType.DMA
    vmem = pl.BlockSpec(memory_space=pltpu.VMEM)
    return pl.pallas_call(
        functools.partial(kernel, chans, wins),
        out_shape=jax.ShapeDtypeStruct((1, 2, rows, chans * rows), BF16),
        in_specs=[vmem] * 4 + [pl.BlockSpec(memory_space=pl.ANY)],
        out_specs=vmem,
        scratch_shapes=[
            pltpu.VMEM(table.shape, F32),
            pltpu.VMEM((rows + 2 * MOST_REACH, width), F32),
            pltpu.VMEM((chans, wins, rows, 2 * width // wins), BF16),
            pltpu.VMEM((wins, rows, 2 * width // wins), BF16),
            dma((TABLE_CUTS,)),
            dma((2,)),
            dma((2,)),
            dma((wins,)),
            dma((wins,)),
            dma((chans,)),
            dma((chans,)),
            dma((chans,)),
            dma((chans,)),
        ],
        compiler_params=pltpu.CompilerParams(
            collective_id=0, has_side_effects=True, vmem_limit_bytes=48 * 2**20
        ),
    )(
        strain.reshape(rows * windows, samples),
        seg_ids.reshape(1, -1),
        dead.reshape(1, -1),
        radius.reshape(1, -1),
        table,
    )


def solution(mesh):
    return jax.shard_map(
        functools.partial(body, mesh.shape["chan"], mesh.shape["win"]),
        mesh=mesh,
        in_specs=(P("chan", "win", None), P(), P(), P("chan")),
        out_specs=P("win", None, "chan", None),
        check_vma=False,
    )
```

```python
import functools

import jax
import jax.numpy as jnp
import numpy as np
from jax import lax
from jax.experimental import pallas as pl
from jax.experimental.pallas import tpu as pltpu
from jax.sharding import PartitionSpec as P

SAMPLES = 1024
FREQ_BINS = 128
FIRST_BIN = 8
SMOOTH_BINS = 4
MOST_REACH = 8
FLOOR_POWER = 0.01
LANES = 128
TABLE_CUTS = 4
GROUP = 8
PEAK = 3.0
TOP_CODE = 32767.0

MESH = pl.DeviceIdType.MESH
F32 = jnp.float32
BF16 = jnp.bfloat16


def fourier_table(bands):
    band_bins = FREQ_BINS // bands
    t = np.arange(SAMPLES, dtype=np.int64)
    bins = FIRST_BIN + np.arange(FREQ_BINS, dtype=np.int64)
    angles = 2.0 * np.pi / SAMPLES * (t[:, None] * bins[None, :] % SAMPLES)
    taper = 0.5 - 0.5 * np.cos(2.0 * np.pi / SAMPLES * (t + 0.5))
    weights = taper[:, None] / np.sqrt(float(SAMPLES))
    cos, sin = weights * np.cos(angles), -weights * np.sin(angles)
    both = np.stack(
        [cos.reshape(SAMPLES, bands, band_bins), sin.reshape(SAMPLES, bands, band_bins)], axis=2
    ).reshape(SAMPLES, 2 * FREQ_BINS)
    return both.astype(np.float32).reshape(TABLE_CUTS, SAMPLES // TABLE_CUTS, -1)


def split3(x):
    high = x.astype(BF16)
    rest = x - high.astype(F32)
    middle = rest.astype(BF16)
    low = (rest - middle.astype(F32)).astype(BF16)
    return high, middle, low


def column_of(row, length, shift=0):
    shape = (length, row.shape[1])
    hit = lax.broadcasted_iota(jnp.int32, shape, 1) == lax.broadcasted_iota(jnp.int32, shape, 0) + shift
    return jnp.sum(jnp.where(hit, row, 0), axis=1, keepdims=True)


def links(seg, dead, radius, me, rows):
    channels, segments = seg.shape[1], dead.shape[1]
    start = me * rows - MOST_REACH
    turned = pltpu.roll(jnp.broadcast_to(seg, (8, channels)), lax.rem(channels - start, channels), 1)
    near = turned[0:1, 0:LANES]
    lane = lax.broadcasted_iota(jnp.int32, (1, LANES), 1)
    inside = (lane + start >= 0) & (lane + start < channels)
    dead_column = column_of(dead, segments)
    is_segment = lax.broadcasted_iota(jnp.int32, (segments, LANES), 0) == near
    dead_near = jnp.sum(jnp.where(is_segment, dead_column, 0), axis=0, keepdims=True)
    alive_near = jnp.where(inside, 1 - dead_near, 0)
    own_segs = column_of(near, rows, MOST_REACH)
    alive_own = column_of(alive_near, rows, MOST_REACH).astype(F32)
    reach = column_of(radius, rows)
    shape = (rows, LANES)
    offsets = lax.broadcasted_iota(jnp.int32, shape, 1) - lax.broadcasted_iota(jnp.int32, shape, 0) - MOST_REACH
    linked = (jnp.abs(offsets) <= reach) & (near == own_segs) & (alive_near > 0)
    linked = jnp.where(linked, 1.0, 0.0)
    counts = jnp.maximum(jnp.sum(linked, axis=1, keepdims=True), 1.0)
    return linked[:, : rows + 2 * MOST_REACH].astype(BF16), alive_own, 1.0 / counts


def bin_of(lanes, bands):
    half = FREQ_BINS // bands
    return lanes // (2 * half) * half + lanes % half


def smoothing(bands):
    shape = (2 * FREQ_BINS, 2 * FREQ_BINS)
    apart = bin_of(lax.broadcasted_iota(jnp.int32, shape, 0), bands) - bin_of(
        lax.broadcasted_iota(jnp.int32, shape, 1), bands
    )
    nearby = jnp.where(jnp.abs(apart) <= SMOOTH_BINS, 1.0, 0.0).astype(BF16)
    bins = bin_of(lax.broadcasted_iota(jnp.int32, (1, 2 * FREQ_BINS), 1), bands)
    members = jnp.minimum(bins + SMOOTH_BINS, FREQ_BINS - 1) - jnp.maximum(bins - SMOOTH_BINS, 0) + 1
    return nearby, 1.0 / members.astype(F32)


def dot(a, b):
    return jnp.dot(a, b, preferred_element_type=F32)


def dot_rows(a, b):
    return lax.dot_general(a, b, (((1,), (1,)), ((), ())), preferred_element_type=F32)


def quantized(x):
    root = jnp.sqrt(jnp.sqrt(jnp.sqrt(jnp.abs(x) * (1.0 / PEAK))))
    code = jnp.minimum(root * TOP_CODE + 0.5, TOP_CODE).astype(jnp.int32)
    return jnp.where(x < 0, -code, code)


def restored(codes):
    y = codes.astype(jnp.int32).astype(F32) * (1.0 / TOP_CODE)
    y2 = y * y
    y4 = y2 * y2
    size = (y4 * y4) * PEAK
    return jnp.where(y < 0, -size, size)


def split2(x):
    high = x.astype(BF16)
    return high, (x - high.astype(F32)).astype(BF16)


def for_each_peer(chans, me, act):
    if chans == GROUP:
        bits = [lax.rem(me // 2**i, 2) for i in range(3)]
        for k in (6, 7, 4, 5, 2, 3, 1):
            act(k, me + sum((1 - 2 * bits[i]) * 2**i for i in range(3) if k >> i & 1))
    else:

        def step(k, carry):
            act(k, lax.rem(me + k, chans))
            return carry

        lax.fori_loop(1, chans, step, 0)


def kernel(
    chans, wins, strain_hbm, seg_hbm, dead_hbm, radius_hbm, table_hbm, out_ref,
    strain, seg, dead, radius, table, ext, blocks, chunks, arrived, load_sem, table_sem,
    halo_send, halo_recv, win_send, win_recv, pair_send, pair_recv,
):
    rows = strain.shape[0]
    width = 2 * FREQ_BINS
    me, win = lax.axis_index("chan"), lax.axis_index("win")

    loads = [
        pltpu.make_async_copy(src, dst, load_sem.at[i])
        for i, (src, dst) in enumerate(
            [(strain_hbm, strain), (seg_hbm, seg), (dead_hbm, dead), (radius_hbm, radius)]
        )
    ]
    table_loads = [
        pltpu.make_async_copy(table_hbm.at[i], table.at[i], table_sem.at[i]) for i in range(TABLE_CUTS)
    ]
    for load in loads + table_loads:
        load.start()

    barrier = pltpu.get_barrier_semaphore()

    def greet(k, peer):
        pl.semaphore_signal(barrier, inc=1, device_id={"chan": peer}, device_id_type=MESH)

    for_each_peer(chans, me, greet)
    for r in range(1, wins):
        pl.semaphore_signal(barrier, inc=1, device_id={"win": lax.rem(win + r, wins)}, device_id_type=MESH)

    nearby, per_member = smoothing(wins)
    for load in loads:
        load.wait()
    linked, alive, per_count = links(seg[...].reshape(1, -1), dead[...], radius[...], me, rows)

    total = None
    cut = SAMPLES // TABLE_CUTS
    for i in range(TABLE_CUTS):
        table_loads[i].wait()
        term = dot(strain[:, i * cut : (i + 1) * cut], jnp.concatenate(split3(table[i]), axis=1))
        total = term if total is None else total + term
    own = total[:, :width] + total[:, width : 2 * width] + total[:, 2 * width :]
    ext[MOST_REACH : MOST_REACH + rows, :] = own

    pl.semaphore_wait(barrier, chans - 1 + wins - 1)

    halos = [
        pltpu.make_async_remote_copy(
            src_ref=ext.at[pl.ds(rows, MOST_REACH)],
            dst_ref=ext.at[pl.ds(0, MOST_REACH)],
            send_sem=halo_send.at[0],
            recv_sem=halo_recv.at[0],
            device_id={"chan": lax.rem(me + 1, chans)},
            device_id_type=MESH,
        ),
        pltpu.make_async_remote_copy(
            src_ref=ext.at[pl.ds(MOST_REACH, MOST_REACH)],
            dst_ref=ext.at[pl.ds(rows + MOST_REACH, MOST_REACH)],
            send_sem=halo_send.at[1],
            recv_sem=halo_recv.at[1],
            device_id={"chan": lax.rem(me + chans - 1, chans)},
            device_id_type=MESH,
        ),
    ]
    for halo in halos:
        halo.start()
    for halo in halos:
        halo.wait_recv()

    sums = dot(linked, jnp.concatenate(split3(ext[...]), axis=1))
    sums = sums[:, :width] + sums[:, width : 2 * width] + sums[:, 2 * width :]
    spectra = alive * (own - sums * per_count)
    smooth = dot(jnp.concatenate(split3(spectra * spectra), axis=0), nearby)
    smooth = (smooth[:rows] + smooth[rows : 2 * rows] + smooth[2 * rows :]) * per_member
    codes = quantized(spectra * lax.rsqrt(jnp.maximum(smooth, FLOOR_POWER)))

    for j in range(wins // 2):
        tile = codes[:, j * LANES : (j + 1) * LANES]
        turned = pltpu.roll(tile, LANES // 2, 1).astype(jnp.int16)
        tile = tile.astype(jnp.int16)
        for h in range(2):
            chunks[h, 2 * j + h] = tile
            chunks[h, 2 * j + 1 - h] = turned

    to_band = []
    for r in range(1, wins):
        band = lax.rem(win + wins - r, wins)
        copy = pltpu.make_async_remote_copy(
            src_ref=chunks.at[r % 2, band],
            dst_ref=arrived.at[r],
            send_sem=win_send.at[r],
            recv_sem=win_recv.at[r],
            device_id={"win": band},
            device_id_type=MESH,
        )
        copy.start()
        to_band.append(copy)

    def piece(owner, peer, k, pair):
        return pltpu.make_async_remote_copy(
            src_ref=blocks.at[pair, owner],
            dst_ref=blocks.at[pair, owner],
            send_sem=pair_send.at[pair, k],
            recv_sem=pair_recv.at[pair, owner],
            device_id={"chan": peer},
            device_id_type=MESH,
        )

    in_first = lax.broadcasted_iota(jnp.int32, (rows, LANES), 1) < LANES // 2
    is_re = lax.broadcasted_iota(jnp.int32, (rows, LANES), 1) % (LANES // 2) < LANES // 4
    pairs = wins // 2
    left = []
    for pair in range(pairs):
        if pair > 0:
            to_band[2 * pair - 1].wait_recv()
        to_band[2 * pair].wait_recv()
        even = chunks[0, win] if pair == 0 else arrived[2 * pair]
        both = jnp.where(in_first, even.astype(jnp.int32), arrived[2 * pair + 1].astype(jnp.int32))
        blocks[pair, me] = both.astype(jnp.int16)
        for_each_peer(chans, me, lambda k, peer: piece(me, peer, k, pair).start())
        x = restored(both)
        after = pltpu.roll(x, LANES - LANES // 4, 1)
        before = pltpu.roll(x, LANES // 4, 1)
        high, low = split2(jnp.concatenate([x, jnp.where(is_re, after, -before)], axis=0))
        left.append(
            jnp.concatenate(
                [
                    jnp.concatenate([high, high], axis=1),
                    jnp.concatenate([low, jnp.zeros_like(low)], axis=1),
                ],
                axis=0,
            )
        )

    scale = 1.0 / FREQ_BINS

    def term(pair, g):
        codes = blocks[pair, pl.ds(g * GROUP, GROUP)].reshape(GROUP * rows, LANES)
        return dot_rows(left[pair], jnp.concatenate(split2(restored(codes)), axis=1))

    def finished(acc):
        return ((acc[: 2 * rows] + acc[2 * rows :]) * scale).astype(out_ref.dtype)

    def wait_pair(pair):
        for_each_peer(chans, me, lambda k, peer: piece(peer, peer, k, pair).wait_recv())

    if chans == GROUP:
        acc = None
        for pair in range(pairs):
            wait_pair(pair)
            acc = term(pair, 0) if acc is None else acc + term(pair, 0)
        out = finished(acc)
        out_ref[0, 0] = out[:rows]
        out_ref[0, 1] = out[rows:]
    else:
        for pair in range(pairs):
            wait_pair(pair)

        @pl.loop(0, chans // GROUP)
        def _(g):
            out = finished(sum(term(pair, g) for pair in range(pairs)))
            at = pl.ds(pl.multiple_of(g * (GROUP * rows), LANES), GROUP * rows)
            out_ref[0, 0, :, at] = out[:rows]
            out_ref[0, 1, :, at] = out[rows:]

    for copy in halos + to_band:
        copy.wait_send()
    for pair in range(pairs):
        for_each_peer(chans, me, lambda k, peer: piece(me, peer, k, pair).wait_send())


def body(chans, wins, strain, seg_ids, dead, radius):
    rows, windows, samples = strain.shape
    table = jnp.asarray(fourier_table(wins))
    width = 2 * FREQ_BINS
    dma = pltpu.SemaphoreType.DMA
    hbm = pl.BlockSpec(memory_space=pltpu.HBM)
    i32, i16 = jnp.int32, jnp.int16
    return pl.pallas_call(
        functools.partial(kernel, chans, wins),
        out_shape=jax.ShapeDtypeStruct((1, 2, rows, chans * rows), BF16),
        in_specs=[hbm] * 5,
        out_specs=pl.BlockSpec(memory_space=pltpu.VMEM),
        scratch_shapes=[
            pltpu.VMEM((rows, samples), BF16),
            pltpu.VMEM(seg_ids.shape, i32),
            pltpu.VMEM((1, dead.shape[0]), i32),
            pltpu.VMEM((1, rows), i32),
            pltpu.VMEM(table.shape, F32),
            pltpu.VMEM((rows + 2 * MOST_REACH, width), F32),
            pltpu.VMEM((wins // 2, chans, rows, LANES), i16),
            pltpu.VMEM((2, wins, rows, LANES), i16),
            pltpu.VMEM((wins, rows, LANES), i16),
            dma((4,)),
            dma((TABLE_CUTS,)),
            dma((2,)),
            dma((2,)),
            dma((wins,)),
            dma((wins,)),
            dma((wins // 2, chans)),
            dma((wins // 2, chans)),
        ],
        compiler_params=pltpu.CompilerParams(
            collective_id=0, has_side_effects=True, vmem_limit_bytes=63 * 2**20
        ),
    )(
        strain.reshape(rows * windows, samples),
        seg_ids,
        dead.reshape(1, -1),
        radius.reshape(1, -1),
        table,
    )


def solution(mesh):
    return jax.shard_map(
        functools.partial(body, mesh.shape["chan"], mesh.shape["win"]),
        mesh=mesh,
        in_specs=(P("chan", "win", None), P(), P(), P("chan")),
        out_specs=P("win", None, "chan", None),
        check_vma=False,
    )
```

```python
import functools

import jax
import jax.numpy as jnp
import numpy as np
from jax import lax
from jax.experimental import pallas as pl
from jax.experimental.pallas import tpu as pltpu
from jax.sharding import PartitionSpec as P

SAMPLES = 1024
FREQ_BINS = 128
FIRST_BIN = 8
SMOOTH_BINS = 4
MOST_REACH = 8
HALO = 16
FLOOR_POWER = 0.01
LANES = 128
TABLE_CUTS = 4
GROUP = 8
PEAK = 3.0
TOP_CODE = 32767.0

MESH = pl.DeviceIdType.MESH
F32 = jnp.float32
BF16 = jnp.bfloat16


def fourier_table(bands):
    band_bins = FREQ_BINS // bands
    t = np.arange(SAMPLES, dtype=np.int64)
    bins = FIRST_BIN + np.arange(FREQ_BINS, dtype=np.int64)
    angles = 2.0 * np.pi / SAMPLES * (t[:, None] * bins[None, :] % SAMPLES)
    taper = 0.5 - 0.5 * np.cos(2.0 * np.pi / SAMPLES * (t + 0.5))
    weights = taper[:, None] / np.sqrt(float(SAMPLES))
    cos, sin = weights * np.cos(angles), -weights * np.sin(angles)
    both = np.stack(
        [cos.reshape(SAMPLES, bands, band_bins), sin.reshape(SAMPLES, bands, band_bins)], axis=2
    ).reshape(SAMPLES, 2 * FREQ_BINS)
    return both.astype(np.float32).reshape(TABLE_CUTS, SAMPLES // TABLE_CUTS, -1)


def split3(x):
    high = x.astype(BF16)
    rest = x - high.astype(F32)
    middle = rest.astype(BF16)
    low = (rest - middle.astype(F32)).astype(BF16)
    return high, middle, low


def column_of(row, length, shift=0):
    shape = (length, row.shape[1])
    hit = lax.broadcasted_iota(jnp.int32, shape, 1) == lax.broadcasted_iota(jnp.int32, shape, 0) + shift
    return jnp.sum(jnp.where(hit, row, 0), axis=1, keepdims=True)


def links(seg, dead, radius, me, rows):
    channels, segments = seg.shape[1], dead.shape[1]
    start = me * rows - HALO
    turned = pltpu.roll(jnp.broadcast_to(seg, (8, channels)), lax.rem(channels - start, channels), 1)
    near = turned[0:1, 0:LANES]
    lane = lax.broadcasted_iota(jnp.int32, (1, LANES), 1)
    inside = (lane + start >= 0) & (lane + start < channels)
    dead_column = column_of(dead, segments)
    is_segment = lax.broadcasted_iota(jnp.int32, (segments, LANES), 0) == near
    dead_near = jnp.sum(jnp.where(is_segment, dead_column, 0), axis=0, keepdims=True)
    alive_near = jnp.where(inside, 1 - dead_near, 0)
    own_segs = column_of(near, rows, HALO)
    alive_own = column_of(alive_near, rows, HALO).astype(F32)
    reach = column_of(radius, rows)
    shape = (rows, LANES)
    offsets = lax.broadcasted_iota(jnp.int32, shape, 1) - lax.broadcasted_iota(jnp.int32, shape, 0) - HALO
    linked = (jnp.abs(offsets) <= reach) & (near == own_segs) & (alive_near > 0)
    linked = jnp.where(linked, 1.0, 0.0)
    counts = jnp.maximum(jnp.sum(linked, axis=1, keepdims=True), 1.0)
    return linked[:, : rows + 2 * HALO].astype(BF16), alive_own, 1.0 / counts


def bin_of(lanes, bands):
    half = FREQ_BINS // bands
    return lanes // (2 * half) * half + lanes % half


def smoothing(bands):
    shape = (2 * FREQ_BINS, 2 * FREQ_BINS)
    apart = bin_of(lax.broadcasted_iota(jnp.int32, shape, 0), bands) - bin_of(
        lax.broadcasted_iota(jnp.int32, shape, 1), bands
    )
    nearby = jnp.where(jnp.abs(apart) <= SMOOTH_BINS, 1.0, 0.0).astype(BF16)
    bins = bin_of(lax.broadcasted_iota(jnp.int32, (1, 2 * FREQ_BINS), 1), bands)
    members = jnp.minimum(bins + SMOOTH_BINS, FREQ_BINS - 1) - jnp.maximum(bins - SMOOTH_BINS, 0) + 1
    return nearby, 1.0 / members.astype(F32)


def dot(a, b):
    return jnp.dot(a, b, preferred_element_type=F32)


def dot_rows(a, b):
    return lax.dot_general(a, b, (((1,), (1,)), ((), ())), preferred_element_type=F32)


def quantized(x):
    root = jnp.sqrt(jnp.sqrt(jnp.sqrt(jnp.abs(x) * (1.0 / PEAK))))
    code = jnp.minimum(root * TOP_CODE + 0.5, TOP_CODE).astype(jnp.int32)
    return jnp.where(x < 0, -code, code)


def restored(codes):
    y = codes.astype(jnp.int32).astype(F32) * (1.0 / TOP_CODE)
    y2 = y * y
    y4 = y2 * y2
    size = (y4 * y4) * PEAK
    return jnp.where(y < 0, -size, size)


def split2(x):
    high = x.astype(BF16)
    return high, (x - high.astype(F32)).astype(BF16)


def for_each_peer(chans, me, act, order=(6, 7, 4, 5, 2, 3, 1)):
    if chans == GROUP:
        bits = [lax.rem(me // 2**i, 2) for i in range(3)]
        for k in order:
            act(k, me + sum((1 - 2 * bits[i]) * 2**i for i in range(3) if k >> i & 1))
    else:

        def step(k, carry):
            act(k, lax.rem(me + k, chans))
            return carry

        lax.fori_loop(1, chans, step, 0)


def kernel(
    chans, wins, strain_hbm, seg_hbm, dead_hbm, radius_hbm, table_hbm, out_ref,
    strain, seg, dead, radius, table, split, blocks, chunks, arrived, right, load_sem, table_sem,
    halo_send, halo_recv, win_send, win_recv, pair_send, pair_recv,
):
    rows = strain_hbm.shape[0]
    width = 2 * FREQ_BINS
    me, win = lax.axis_index("chan"), lax.axis_index("win")

    loads = [
        pltpu.make_async_copy(src, dst, load_sem.at[i])
        for i, (src, dst) in enumerate(
            [(strain_hbm, strain.at[pl.ds(HALO, rows)]), (seg_hbm, seg), (dead_hbm, dead), (radius_hbm, radius)]
        )
    ]
    table_loads = [
        pltpu.make_async_copy(table_hbm.at[i], table.at[i], table_sem.at[i]) for i in range(TABLE_CUTS)
    ]
    for load in loads + table_loads:
        load.start()

    barrier = pltpu.get_barrier_semaphore()

    def greet(k, peer):
        pl.semaphore_signal(barrier, inc=1, device_id={"chan": peer}, device_id_type=MESH)

    for_each_peer(chans, me, greet)
    for r in range(1, wins):
        pl.semaphore_signal(barrier, inc=1, device_id={"win": lax.rem(win + r, wins)}, device_id_type=MESH)

    pl.semaphore_wait(barrier, chans - 1 + wins - 1)

    halos = [
        pltpu.make_async_remote_copy(
            src_ref=strain_hbm.at[pl.ds(rows - HALO, HALO)],
            dst_ref=strain.at[pl.ds(0, HALO)],
            send_sem=halo_send.at[0],
            recv_sem=halo_recv.at[0],
            device_id={"chan": lax.rem(me + 1, chans)},
            device_id_type=MESH,
        ),
        pltpu.make_async_remote_copy(
            src_ref=strain_hbm.at[pl.ds(0, HALO)],
            dst_ref=strain.at[pl.ds(rows + HALO, HALO)],
            send_sem=halo_send.at[1],
            recv_sem=halo_recv.at[1],
            device_id={"chan": lax.rem(me + chans - 1, chans)},
            device_id_type=MESH,
        ),
    ]
    for halo in halos:
        halo.start()

    nearby, per_member = smoothing(wins)
    for load in loads:
        load.wait()
    linked, alive, per_count = links(seg[...].reshape(1, -1), dead[...], radius[...], me, rows)
    for i in range(TABLE_CUTS):
        table_loads[i].wait()
        for part, value in enumerate(split3(table[i])):
            split[i, :, part * width : (part + 1) * width] = value
    for halo in halos:
        halo.wait_recv()

    total = None
    cut = SAMPLES // TABLE_CUTS
    for i in range(TABLE_CUTS):
        term = dot(strain[:, i * cut : (i + 1) * cut], split[i])
        total = term if total is None else total + term
    total = total[:, :width] + total[:, width : 2 * width] + total[:, 2 * width :]
    sums = dot(linked, jnp.concatenate(split3(total), axis=1))
    sums = sums[:, :width] + sums[:, width : 2 * width] + sums[:, 2 * width :]
    spectra = alive * (total[HALO : HALO + rows] - sums * per_count)
    smooth = dot(jnp.concatenate(split3(spectra * spectra), axis=0), nearby)
    smooth = (smooth[:rows] + smooth[rows : 2 * rows] + smooth[2 * rows :]) * per_member
    codes = quantized(spectra * lax.rsqrt(jnp.maximum(smooth, FLOOR_POWER)))

    for j in range(wins // 2):
        tile = codes[:, j * LANES : (j + 1) * LANES]
        turned = pltpu.roll(tile, LANES // 2, 1).astype(jnp.int16)
        tile = tile.astype(jnp.int16)
        for h in range(2):
            chunks[h, 2 * j + h] = tile
            chunks[h, 2 * j + 1 - h] = turned

    to_band = []
    for r in range(1, wins):
        band = lax.rem(win + wins - r, wins)
        copy = pltpu.make_async_remote_copy(
            src_ref=chunks.at[r % 2, band],
            dst_ref=arrived.at[r],
            send_sem=win_send.at[r],
            recv_sem=win_recv.at[r],
            device_id={"win": band},
            device_id_type=MESH,
        )
        copy.start()
        to_band.append(copy)

    def piece(owner, peer, k, pair):
        return pltpu.make_async_remote_copy(
            src_ref=blocks.at[pair, owner],
            dst_ref=blocks.at[pair, owner],
            send_sem=pair_send.at[pair, k],
            recv_sem=pair_recv.at[pair, owner],
            device_id={"chan": peer},
            device_id_type=MESH,
        )

    in_first = lax.broadcasted_iota(jnp.int32, (rows, LANES), 1) < LANES // 2
    is_re = lax.broadcasted_iota(jnp.int32, (rows, LANES), 1) % (LANES // 2) < LANES // 4
    pairs = wins // 2
    left = []
    for pair in range(pairs):
        if pair > 0:
            to_band[2 * pair - 1].wait_recv()
        to_band[2 * pair].wait_recv()
        even = chunks[0, win] if pair == 0 else arrived[2 * pair]
        both = jnp.where(in_first, even.astype(jnp.int32), arrived[2 * pair + 1].astype(jnp.int32))
        blocks[pair, me] = both.astype(jnp.int16)
        for_each_peer(chans, me, lambda k, peer: piece(me, peer, k, pair).start())
        x = restored(both)
        right[pair, me] = jnp.concatenate(split2(x), axis=1)
        after = pltpu.roll(x, LANES - LANES // 4, 1)
        before = pltpu.roll(x, LANES // 4, 1)
        high, low = split2(jnp.concatenate([x, jnp.where(is_re, after, -before)], axis=0))
        left.append(
            jnp.concatenate(
                [
                    jnp.concatenate([high, high], axis=1),
                    jnp.concatenate([low, jnp.zeros_like(low)], axis=1),
                ],
                axis=0,
            )
        )

    scale = 1.0 / FREQ_BINS

    def term(pair, g):
        return dot_rows(left[pair], right[pair, pl.ds(g * GROUP, GROUP)].reshape(GROUP * rows, 2 * LANES))

    def finished(acc):
        return ((acc[: 2 * rows] + acc[2 * rows :]) * scale).astype(out_ref.dtype)

    def take(pair, k, peer):
        piece(peer, peer, k, pair).wait_recv()
        right[pair, peer] = jnp.concatenate(split2(restored(blocks[pair, peer])), axis=1)

    def take_pair(pair):
        for_each_peer(chans, me, functools.partial(take, pair), (1, 2, 3, 4, 5, 6, 7))

    if chans == GROUP:
        acc = None
        for pair in range(pairs):
            take_pair(pair)
            acc = term(pair, 0) if acc is None else acc + term(pair, 0)
        out = finished(acc)
        out_ref[0, 0] = out[:rows]
        out_ref[0, 1] = out[rows:]
    else:
        for pair in range(pairs):
            take_pair(pair)

        @pl.loop(0, chans // GROUP)
        def _(g):
            out = finished(sum(term(pair, g) for pair in range(pairs)))
            at = pl.ds(pl.multiple_of(g * (GROUP * rows), LANES), GROUP * rows)
            out_ref[0, 0, :, at] = out[:rows]
            out_ref[0, 1, :, at] = out[rows:]

    for copy in halos + to_band:
        copy.wait_send()
    for pair in range(pairs):
        for_each_peer(chans, me, lambda k, peer: piece(me, peer, k, pair).wait_send())


def body(chans, wins, strain, seg_ids, dead, radius):
    rows, windows, samples = strain.shape
    table = jnp.asarray(fourier_table(wins))
    width = 2 * FREQ_BINS
    dma = pltpu.SemaphoreType.DMA
    hbm = pl.BlockSpec(memory_space=pltpu.HBM)
    i32, i16 = jnp.int32, jnp.int16
    return pl.pallas_call(
        functools.partial(kernel, chans, wins),
        out_shape=pltpu.VMEM((1, 2, rows, chans * rows), BF16),
        in_specs=[hbm] * 5,
        out_specs=pl.BlockSpec(memory_space=pltpu.VMEM),
        scratch_shapes=[
            pltpu.VMEM((rows + 2 * HALO, samples), BF16),
            pltpu.VMEM(seg_ids.shape, i32),
            pltpu.VMEM((1, dead.shape[0]), i32),
            pltpu.VMEM((1, rows), i32),
            pltpu.VMEM(table.shape, F32),
            pltpu.VMEM(table.shape[:2] + (3 * width,), BF16),
            pltpu.VMEM((wins // 2, chans, rows, LANES), i16),
            pltpu.VMEM((2, wins, rows, LANES), i16),
            pltpu.VMEM((wins, rows, LANES), i16),
            pltpu.VMEM((wins // 2, chans, rows, 2 * LANES), BF16),
            dma((4,)),
            dma((TABLE_CUTS,)),
            dma((2,)),
            dma((2,)),
            dma((wins,)),
            dma((wins,)),
            dma((wins // 2, chans)),
            dma((wins // 2, chans)),
        ],
        compiler_params=pltpu.CompilerParams(
            collective_id=0, has_side_effects=True, vmem_limit_bytes=(63 if chans == GROUP else 48) * 2**20
        ),
    )(
        strain.reshape(rows * windows, samples),
        seg_ids,
        dead.reshape(1, -1),
        radius.reshape(1, -1),
        table,
    )


def solution(mesh):
    return jax.shard_map(
        functools.partial(body, mesh.shape["chan"], mesh.shape["win"]),
        mesh=mesh,
        in_specs=(P("chan", "win", None), P(), P(), P("chan")),
        out_specs=P("win", None, "chan", None),
        check_vma=False,
    )
```

```python
import functools

import jax
import jax.numpy as jnp
import numpy as np
from jax import lax
from jax.experimental import pallas as pl
from jax.experimental.pallas import tpu as pltpu
from jax.sharding import PartitionSpec as P

SAMPLES = 1024
FREQ_BINS = 128
FIRST_BIN = 8
SMOOTH_BINS = 4
MOST_REACH = 8
HALO = 16
FLOOR_POWER = 0.01
LANES = 128
TABLE_CUTS = 4
GROUP = 8
PEAK = 3.0
TOP_CODE = 32767.0

MESH = pl.DeviceIdType.MESH
F32 = jnp.float32
BF16 = jnp.bfloat16


def fourier_table(bands):
    band_bins = FREQ_BINS // bands
    t = np.arange(SAMPLES, dtype=np.int64)
    bins = FIRST_BIN + np.arange(FREQ_BINS, dtype=np.int64)
    angles = 2.0 * np.pi / SAMPLES * (t[:, None] * bins[None, :] % SAMPLES)
    taper = 0.5 - 0.5 * np.cos(2.0 * np.pi / SAMPLES * (t + 0.5))
    weights = taper[:, None] / np.sqrt(float(SAMPLES))
    cos, sin = weights * np.cos(angles), -weights * np.sin(angles)
    both = np.stack(
        [cos.reshape(SAMPLES, bands, band_bins), sin.reshape(SAMPLES, bands, band_bins)], axis=2
    ).reshape(SAMPLES, 2 * FREQ_BINS)
    return both.astype(np.float32).reshape(TABLE_CUTS, SAMPLES // TABLE_CUTS, -1)


def split3(x):
    high = x.astype(BF16)
    rest = x - high.astype(F32)
    middle = rest.astype(BF16)
    low = (rest - middle.astype(F32)).astype(BF16)
    return high, middle, low


def column_of(row, length, shift=0):
    shape = (length, row.shape[1])
    hit = lax.broadcasted_iota(jnp.int32, shape, 1) == lax.broadcasted_iota(jnp.int32, shape, 0) + shift
    return jnp.sum(jnp.where(hit, row, 0), axis=1, keepdims=True)


def links(seg, dead, radius, me, rows):
    channels, segments = seg.shape[1], dead.shape[1]
    start = me * rows - HALO
    turned = pltpu.roll(jnp.broadcast_to(seg, (8, channels)), lax.rem(channels - start, channels), 1)
    near = turned[0:1, 0:LANES]
    lane = lax.broadcasted_iota(jnp.int32, (1, LANES), 1)
    inside = (lane + start >= 0) & (lane + start < channels)
    dead_column = column_of(dead, segments)
    is_segment = lax.broadcasted_iota(jnp.int32, (segments, LANES), 0) == near
    dead_near = jnp.sum(jnp.where(is_segment, dead_column, 0), axis=0, keepdims=True)
    alive_near = jnp.where(inside, 1 - dead_near, 0)
    own_segs = column_of(near, rows, HALO)
    alive_own = column_of(alive_near, rows, HALO).astype(F32)
    reach = column_of(radius, rows)
    shape = (rows, LANES)
    offsets = lax.broadcasted_iota(jnp.int32, shape, 1) - lax.broadcasted_iota(jnp.int32, shape, 0) - HALO
    linked = (jnp.abs(offsets) <= reach) & (near == own_segs) & (alive_near > 0)
    linked = jnp.where(linked, 1.0, 0.0)
    counts = jnp.maximum(jnp.sum(linked, axis=1, keepdims=True), 1.0)
    return linked[:, : rows + 2 * HALO].astype(BF16), alive_own, 1.0 / counts


def bin_of(lanes, bands):
    half = FREQ_BINS // bands
    return lanes // (2 * half) * half + lanes % half


def smoothing(bands):
    lanes = 2 * FREQ_BINS
    bins = bin_of(lax.broadcasted_iota(jnp.int32, (1, lanes), 1), bands)
    apart = bin_of(lax.broadcasted_iota(jnp.int32, (lanes, 1), 0), bands) - bins
    nearby = jnp.where(jnp.abs(apart) <= SMOOTH_BINS, 1.0, 0.0).astype(BF16)
    members = jnp.minimum(bins + SMOOTH_BINS, FREQ_BINS - 1) - jnp.maximum(bins - SMOOTH_BINS, 0) + 1
    return nearby, 1.0 / members.astype(F32)


def dot(a, b):
    return jnp.dot(a, b, preferred_element_type=F32)


def dot_rows(a, b):
    return lax.dot_general(a, b, (((1,), (1,)), ((), ())), preferred_element_type=F32)


def quantized(x):
    root = jnp.sqrt(jnp.sqrt(jnp.sqrt(jnp.abs(x) * (1.0 / PEAK))))
    code = jnp.minimum(root * TOP_CODE + 0.5, TOP_CODE).astype(jnp.int32)
    return jnp.where(x < 0, -code, code)


def restored(codes):
    y = codes.astype(jnp.int32).astype(F32) * (1.0 / TOP_CODE)
    y2 = y * y
    y4 = y2 * y2
    size = (y4 * y4) * PEAK
    return jnp.where(y < 0, -size, size)


def split2(x):
    high = x.astype(BF16)
    return high, (x - high.astype(F32)).astype(BF16)


def for_each_peer(chans, me, act, far_first=True):
    def step(i, carry):
        k = chans - 1 - i if far_first else i + 1
        peer, bit = me, 1
        while bit < chans:
            peer = peer + (k // bit % 2) * (1 - 2 * (me // bit % 2)) * bit
            bit *= 2
        act(k, peer if bit == chans else lax.rem(me + k, chans))
        return carry

    lax.fori_loop(0, chans - 1, step, 0)


def kernel(
    chans, wins, strain_hbm, seg_hbm, dead_hbm, radius_hbm, table_hbm, out_ref,
    strain, seg, dead, radius, table, split, blocks, chunks, arrived, right, load_sem, table_sem,
    halo_send, halo_recv, win_send, win_recv, pair_send, pair_recv,
):
    rows = strain_hbm.shape[0]
    width = 2 * FREQ_BINS
    me, win = lax.axis_index("chan"), lax.axis_index("win")

    loads = [
        pltpu.make_async_copy(src, dst, load_sem.at[i])
        for i, (src, dst) in enumerate(
            [(strain_hbm, strain.at[pl.ds(HALO, rows)]), (seg_hbm, seg), (dead_hbm, dead), (radius_hbm, radius)]
        )
    ]
    table_loads = [
        pltpu.make_async_copy(table_hbm.at[i], table.at[i], table_sem.at[i]) for i in range(TABLE_CUTS)
    ]
    for load in loads + table_loads:
        load.start()

    barrier = pltpu.get_barrier_semaphore()

    def greet(k, peer):
        pl.semaphore_signal(barrier, inc=1, device_id={"chan": peer}, device_id_type=MESH)

    for_each_peer(chans, me, greet)
    for r in range(1, wins):
        pl.semaphore_signal(barrier, inc=1, device_id={"win": lax.rem(win + r, wins)}, device_id_type=MESH)

    pl.semaphore_wait(barrier, chans - 1 + wins - 1)

    halos = [
        pltpu.make_async_remote_copy(
            src_ref=strain_hbm.at[pl.ds(rows - HALO, HALO)],
            dst_ref=strain.at[pl.ds(0, HALO)],
            send_sem=halo_send.at[0],
            recv_sem=halo_recv.at[0],
            device_id={"chan": lax.rem(me + 1, chans)},
            device_id_type=MESH,
        ),
        pltpu.make_async_remote_copy(
            src_ref=strain_hbm.at[pl.ds(0, HALO)],
            dst_ref=strain.at[pl.ds(rows + HALO, HALO)],
            send_sem=halo_send.at[1],
            recv_sem=halo_recv.at[1],
            device_id={"chan": lax.rem(me + chans - 1, chans)},
            device_id_type=MESH,
        ),
    ]
    for halo in halos:
        halo.start()

    nearby, per_member = smoothing(wins)
    for load in loads:
        load.wait()
    linked, alive, per_count = links(seg[...].reshape(1, -1), dead[...], radius[...], me, rows)

    @pl.loop(0, TABLE_CUTS)
    def _(i):
        pltpu.make_async_copy(table_hbm.at[i], table.at[i], table_sem.at[i]).wait()
        for part, value in enumerate(split3(table[i])):
            split[i, :, part * width : (part + 1) * width] = value

    for halo in halos:
        halo.wait_recv()

    cut = SAMPLES // TABLE_CUTS

    def transform(i, total):
        term = dot(strain[:, pl.ds(pl.multiple_of(i * cut, cut), cut)], split[i])
        return total + (term[:, :width] + term[:, width : 2 * width] + term[:, 2 * width :])

    total = lax.fori_loop(0, TABLE_CUTS, transform, jnp.zeros((rows + 2 * HALO, width), F32))
    sums = dot(linked, jnp.concatenate(split3(total), axis=1))
    sums = sums[:, :width] + sums[:, width : 2 * width] + sums[:, 2 * width :]
    spectra = alive * (total[HALO : HALO + rows] - sums * per_count)
    smooth = dot(jnp.concatenate(split3(spectra * spectra), axis=0), nearby)
    smooth = (smooth[:rows] + smooth[rows : 2 * rows] + smooth[2 * rows :]) * per_member
    codes = quantized(spectra * lax.rsqrt(jnp.maximum(smooth, FLOOR_POWER)))

    for j in range(wins // 2):
        tile = codes[:, j * LANES : (j + 1) * LANES]
        turned = pltpu.roll(tile, LANES // 2, 1).astype(jnp.int16)
        tile = tile.astype(jnp.int16)
        for h in range(2):
            chunks[h, 2 * j + h] = tile
            chunks[h, 2 * j + 1 - h] = turned

    to_band = []
    for r in range(1, wins):
        band = lax.rem(win + wins - r, wins)
        copy = pltpu.make_async_remote_copy(
            src_ref=chunks.at[r % 2, band],
            dst_ref=arrived.at[r],
            send_sem=win_send.at[r],
            recv_sem=win_recv.at[r],
            device_id={"win": band},
            device_id_type=MESH,
        )
        copy.start()
        to_band.append(copy)

    def piece(owner, peer, k, pair):
        return pltpu.make_async_remote_copy(
            src_ref=blocks.at[pair, owner],
            dst_ref=blocks.at[pair, owner],
            send_sem=pair_send.at[pair, k],
            recv_sem=pair_recv.at[pair, owner],
            device_id={"chan": peer},
            device_id_type=MESH,
        )

    in_first = lax.broadcasted_iota(jnp.int32, (rows, LANES), 1) < LANES // 2
    is_re = lax.broadcasted_iota(jnp.int32, (rows, LANES), 1) % (LANES // 2) < LANES // 4
    pairs = wins // 2
    left = []
    for pair in range(pairs):
        if pair > 0:
            to_band[2 * pair - 1].wait_recv()
        to_band[2 * pair].wait_recv()
        even = chunks[0, win] if pair == 0 else arrived[2 * pair]
        both = jnp.where(in_first, even.astype(jnp.int32), arrived[2 * pair + 1].astype(jnp.int32))
        blocks[pair, me] = both.astype(jnp.int16)
        for_each_peer(chans, me, lambda k, peer: piece(me, peer, k, pair).start())
        x = restored(both)
        right[pair, me] = jnp.concatenate(split2(x), axis=1)
        after = pltpu.roll(x, LANES - LANES // 4, 1)
        before = pltpu.roll(x, LANES // 4, 1)
        high, low = split2(jnp.concatenate([x, jnp.where(is_re, after, -before)], axis=0))
        left.append(
            jnp.concatenate(
                [
                    jnp.concatenate([high, high], axis=1),
                    jnp.concatenate([low, jnp.zeros_like(low)], axis=1),
                ],
                axis=0,
            )
        )

    scale = 1.0 / FREQ_BINS

    def term(pair, g):
        return dot_rows(left[pair], right[pair, pl.ds(g * GROUP, GROUP)].reshape(GROUP * rows, 2 * LANES))

    def finished(acc):
        return ((acc[: 2 * rows] + acc[2 * rows :]) * scale).astype(out_ref.dtype)

    def take(pair, k, peer):
        piece(peer, peer, k, pair).wait_recv()
        right[pair, peer] = jnp.concatenate(split2(restored(blocks[pair, peer])), axis=1)

    def take_pair(pair):
        for_each_peer(chans, me, functools.partial(take, pair), False)

    if chans == GROUP:
        acc = None
        for pair in range(pairs):
            take_pair(pair)
            acc = term(pair, 0) if acc is None else acc + term(pair, 0)
        out = finished(acc)
        out_ref[0, 0] = out[:rows]
        out_ref[0, 1] = out[rows:]
    else:
        for pair in range(pairs):
            take_pair(pair)

        @pl.loop(0, chans // GROUP)
        def _(g):
            out = finished(sum(term(pair, g) for pair in range(pairs)))
            at = pl.ds(pl.multiple_of(g * (GROUP * rows), LANES), GROUP * rows)
            out_ref[0, 0, :, at] = out[:rows]
            out_ref[0, 1, :, at] = out[rows:]

    for copy in halos + to_band:
        copy.wait_send()
    for pair in range(pairs):
        for_each_peer(chans, me, lambda k, peer: piece(me, peer, k, pair).wait_send())


def body(chans, wins, strain, seg_ids, dead, radius):
    rows, windows, samples = strain.shape
    table = jnp.asarray(fourier_table(wins))
    width = 2 * FREQ_BINS
    dma = pltpu.SemaphoreType.DMA
    hbm = pl.BlockSpec(memory_space=pltpu.HBM)
    i32, i16 = jnp.int32, jnp.int16
    return pl.pallas_call(
        functools.partial(kernel, chans, wins),
        out_shape=pltpu.VMEM((1, 2, rows, chans * rows), BF16),
        in_specs=[hbm] * 5,
        out_specs=pl.BlockSpec(memory_space=pltpu.VMEM),
        scratch_shapes=[
            pltpu.VMEM((rows + 2 * HALO, samples), BF16),
            pltpu.VMEM(seg_ids.shape, i32),
            pltpu.VMEM((1, dead.shape[0]), i32),
            pltpu.VMEM((1, rows), i32),
            pltpu.VMEM(table.shape, F32),
            pltpu.VMEM(table.shape[:2] + (3 * width,), BF16),
            pltpu.VMEM((wins // 2, chans, rows, LANES), i16),
            pltpu.VMEM((2, wins, rows, LANES), i16),
            pltpu.VMEM((wins, rows, LANES), i16),
            pltpu.VMEM((wins // 2, chans, rows, 2 * LANES), BF16),
            dma((4,)),
            dma((TABLE_CUTS,)),
            dma((2,)),
            dma((2,)),
            dma((wins,)),
            dma((wins,)),
            dma((wins // 2, chans)),
            dma((wins // 2, chans)),
        ],
        compiler_params=pltpu.CompilerParams(
            collective_id=0, has_side_effects=True, vmem_limit_bytes=(63 if chans == GROUP else 48) * 2**20
        ),
    )(
        strain.reshape(rows * windows, samples),
        seg_ids,
        dead.reshape(1, -1),
        radius.reshape(1, -1),
        table,
    )


def solution(mesh):
    return jax.shard_map(
        functools.partial(body, mesh.shape["chan"], mesh.shape["win"]),
        mesh=mesh,
        in_specs=(P("chan", "win", None), P(), P(), P("chan")),
        out_specs=P("win", None, "chan", None),
        check_vma=False,
    )
```

```python
import functools
import math

import jax
import jax.numpy as jnp
import numpy as np
from jax import lax
from jax.experimental import pallas as pl
from jax.experimental.pallas import tpu as pltpu
from jax.sharding import PartitionSpec as P

SAMPLES = 1024
FREQ_BINS = 128
FIRST_BIN = 8
SMOOTH_BINS = 4
MOST_REACH = 8
FLOOR_POWER = 0.01
LANES = 128
TABLE_CUTS = 4
GROUP = 8
PEAK = 3.0
TOP_CODE = 32767.0
ROOT_SCALE = math.log2(TOP_CODE) - math.log2(PEAK) / 8.0

MESH = pl.DeviceIdType.MESH
F32 = jnp.float32
BF16 = jnp.bfloat16


def fourier_table(bands):
    band_bins = FREQ_BINS // bands
    t = np.arange(SAMPLES, dtype=np.int64)
    bins = FIRST_BIN + np.arange(FREQ_BINS, dtype=np.int64)
    angles = 2.0 * np.pi / SAMPLES * (t[:, None] * bins[None, :] % SAMPLES)
    taper = 0.5 - 0.5 * np.cos(2.0 * np.pi / SAMPLES * (t + 0.5))
    weights = taper[:, None] / np.sqrt(float(SAMPLES))
    cos, sin = weights * np.cos(angles), -weights * np.sin(angles)
    both = np.stack(
        [cos.reshape(SAMPLES, bands, band_bins), sin.reshape(SAMPLES, bands, band_bins)], axis=2
    ).reshape(SAMPLES, 2 * FREQ_BINS)
    return both.astype(np.float32).reshape(TABLE_CUTS, SAMPLES // TABLE_CUTS, -1)


def split3(x):
    high = x.astype(BF16)
    rest = x - high.astype(F32)
    middle = rest.astype(BF16)
    low = (rest - middle.astype(F32)).astype(BF16)
    return high, middle, low


def column_of(row, length, shift=0):
    shape = (length, row.shape[1])
    hit = lax.broadcasted_iota(jnp.int32, shape, 1) == lax.broadcasted_iota(jnp.int32, shape, 0) + shift
    return jnp.sum(jnp.where(hit, row, 0), axis=1, keepdims=True)


def links(seg, dead, radius, me, rows):
    channels, segments = seg.shape[1], dead.shape[1]
    start = me * rows - MOST_REACH
    turned = pltpu.roll(jnp.broadcast_to(seg, (8, channels)), lax.rem(channels - start, channels), 1)
    near = turned[0:1, 0:LANES]
    lane = lax.broadcasted_iota(jnp.int32, (1, LANES), 1)
    inside = (lane + start >= 0) & (lane + start < channels)
    dead_column = column_of(dead, segments)
    is_segment = lax.broadcasted_iota(jnp.int32, (segments, LANES), 0) == near
    dead_near = jnp.sum(jnp.where(is_segment, dead_column, 0), axis=0, keepdims=True)
    alive_near = jnp.where(inside, 1 - dead_near, 0)
    own_segs = column_of(near, rows, MOST_REACH)
    alive_own = column_of(alive_near, rows, MOST_REACH).astype(F32)
    reach = column_of(radius, rows)
    shape = (rows, LANES)
    offsets = lax.broadcasted_iota(jnp.int32, shape, 1) - lax.broadcasted_iota(jnp.int32, shape, 0) - MOST_REACH
    linked = (jnp.abs(offsets) <= reach) & (near == own_segs) & (alive_near > 0)
    linked = jnp.where(linked, 1.0, 0.0)
    counts = jnp.maximum(jnp.sum(linked, axis=1, keepdims=True), 1.0)
    lane = lax.broadcasted_iota(jnp.int32, shape, 1)
    own_first = pltpu.roll(linked, LANES - MOST_REACH, 1)
    linked = jnp.where(lane < rows, own_first, jnp.where(lane < rows + MOST_REACH, pltpu.roll(linked, rows, 1), linked))
    return linked[:, : rows + 2 * MOST_REACH].astype(BF16), alive_own, 1.0 / counts


def bin_of(lanes, bands):
    half = FREQ_BINS // bands
    return lanes // (2 * half) * half + lanes % half


def smoothing(bands):
    lanes = 2 * FREQ_BINS
    bins = bin_of(lax.broadcasted_iota(jnp.int32, (1, lanes), 1), bands)
    apart = bin_of(lax.broadcasted_iota(jnp.int32, (lanes, 1), 0), bands) - bins
    nearby = jnp.where(jnp.abs(apart) <= SMOOTH_BINS, 1.0, 0.0).astype(BF16)
    members = jnp.minimum(bins + SMOOTH_BINS, FREQ_BINS - 1) - jnp.maximum(bins - SMOOTH_BINS, 0) + 1
    return nearby, 1.0 / members.astype(F32)


def dot(a, b):
    return jnp.dot(a, b, preferred_element_type=F32)


def dot_rows(a, b):
    return lax.dot_general(a, b, (((1,), (1,)), ((), ())), preferred_element_type=F32)


def quantized(x, power, mean_power):
    root = jnp.exp2((jnp.log2(power) - jnp.log2(mean_power)) * 0.0625 + ROOT_SCALE)
    code = jnp.minimum(root + 0.5, TOP_CODE).astype(jnp.int32)
    return jnp.where(x < 0, -code, code)


def restored(codes):
    y = codes.astype(jnp.int32).astype(F32) * (1.0 / TOP_CODE)
    y2 = y * y
    y4 = y2 * y2
    size = (y4 * y4) * PEAK
    return jnp.where(y < 0, -size, size)


def split2(x):
    high = x.astype(BF16)
    return high, (x - high.astype(F32)).astype(BF16)


def for_each_peer(chans, me, act, order=(6, 7, 4, 5, 2, 3, 1)):
    if chans == GROUP:
        bits = [lax.rem(me // 2**i, 2) for i in range(3)]
        for k in order:
            act(k, me + sum((1 - 2 * bits[i]) * 2**i for i in range(3) if k >> i & 1))
    else:

        def step(k, carry):
            act(k, lax.rem(me + k, chans))
            return carry

        lax.fori_loop(1, chans, step, 0)


def kernel(
    chans, wins, strain_hbm, seg_hbm, dead_hbm, radius_hbm, table_hbm, out_ref,
    strain, seg, dead, radius, table, edges, halo_rows, blocks, chunks, arrived, right, load_sem, table_sem,
    halo_send, halo_recv, win_send, win_recv, pair_send, pair_recv,
):
    rows = strain_hbm.shape[0]
    width = 2 * FREQ_BINS
    me, win = lax.axis_index("chan"), lax.axis_index("win")

    barrier = pltpu.get_barrier_semaphore()

    def greet(k, peer):
        pl.semaphore_signal(barrier, inc=1, device_id={"chan": peer}, device_id_type=MESH)

    for_each_peer(chans, me, greet)
    for r in range(1, wins):
        pl.semaphore_signal(barrier, inc=1, device_id={"win": lax.rem(win + r, wins)}, device_id_type=MESH)

    loads = [
        pltpu.make_async_copy(src, dst, load_sem.at[i])
        for i, (src, dst) in enumerate(
            [(strain_hbm, strain), (seg_hbm, seg), (dead_hbm, dead), (radius_hbm, radius)]
        )
    ]
    table_loads = [
        pltpu.make_async_copy(table_hbm.at[i], table.at[i], table_sem.at[i]) for i in range(TABLE_CUTS)
    ]
    for load in loads + table_loads:
        load.start()

    nearby, per_member = smoothing(wins)
    for load in loads:
        load.wait()
    linked, alive, per_count = links(seg[...].reshape(1, -1), dead[...], radius[...], me, rows)

    total = None
    cut = SAMPLES // TABLE_CUTS
    for i in range(TABLE_CUTS):
        table_loads[i].wait()
        term = dot(strain[:, i * cut : (i + 1) * cut], jnp.concatenate(split3(table[i]), axis=1))
        total = term if total is None else total + term
    own = total[:, :width] + total[:, width : 2 * width] + total[:, 2 * width :]
    edges[0] = own[rows - MOST_REACH :]
    edges[1] = own[:MOST_REACH]
    own_parts = jnp.concatenate(split3(own), axis=1)

    pl.semaphore_wait(barrier, chans - 1 + wins - 1)

    halos = [
        pltpu.make_async_remote_copy(
            src_ref=edges.at[side],
            dst_ref=halo_rows.at[side],
            send_sem=halo_send.at[side],
            recv_sem=halo_recv.at[side],
            device_id={"chan": lax.rem(me + step, chans)},
            device_id_type=MESH,
        )
        for side, step in enumerate((1, chans - 1))
    ]
    for halo in halos:
        halo.start()
    for halo in halos:
        halo.wait_recv()

    near_rows = halo_rows[...].reshape(2 * MOST_REACH, width)
    near_parts = jnp.concatenate(split3(near_rows), axis=1)
    sums = dot(linked, jnp.concatenate([own_parts, near_parts], axis=0))
    sums = sums[:, :width] + sums[:, width : 2 * width] + sums[:, 2 * width :]
    spectra = alive * (own - sums * per_count)
    power = spectra * spectra
    smooth = dot(jnp.concatenate(split3(power), axis=0), nearby)
    smooth = (smooth[:rows] + smooth[rows : 2 * rows] + smooth[2 * rows :]) * per_member
    codes = quantized(spectra, power, jnp.maximum(smooth, FLOOR_POWER))

    for j in range(wins // 2):
        tile = codes[:, j * LANES : (j + 1) * LANES]
        turned = pltpu.roll(tile, LANES // 2, 1).astype(jnp.int16)
        tile = tile.astype(jnp.int16)
        for h in range(2):
            chunks[h, 2 * j + h] = tile
            chunks[h, 2 * j + 1 - h] = turned

    to_band = {}
    for r in range(1, wins):
        band = win + sum((1 - 2 * lax.rem(win // 2**i, 2)) * 2**i for i in range(2) if r >> i & 1)
        copy = pltpu.make_async_remote_copy(
            src_ref=chunks.at[r % 2, band],
            dst_ref=arrived.at[r],
            send_sem=win_send.at[r],
            recv_sem=win_recv.at[r],
            device_id={"win": band},
            device_id_type=MESH,
        )
        copy.start()
        to_band[r] = copy

    def piece(owner, peer, k, pair):
        return pltpu.make_async_remote_copy(
            src_ref=blocks.at[pair, owner],
            dst_ref=blocks.at[pair, owner],
            send_sem=pair_send.at[pair, k],
            recv_sem=pair_recv.at[pair, owner],
            device_id={"chan": peer},
            device_id_type=MESH,
        )

    in_first = lax.broadcasted_iota(jnp.int32, (rows, LANES), 1) < LANES // 2
    is_re = lax.broadcasted_iota(jnp.int32, (rows, LANES), 1) % (LANES // 2) < LANES // 4
    pairs = wins // 2
    left = []
    for pair in range(pairs):
        if pair > 0:
            to_band[2 * pair].wait_recv()
        to_band[2 * pair + 1].wait_recv()
        even = chunks[0, win] if pair == 0 else arrived[2 * pair]
        both = jnp.where(in_first, even.astype(jnp.int32), arrived[2 * pair + 1].astype(jnp.int32))
        blocks[pair, me] = both.astype(jnp.int16)
        for_each_peer(chans, me, lambda k, peer: piece(me, peer, k, pair).start())
        x = restored(both)
        right[pair, me] = jnp.concatenate(split2(x), axis=1)
        after = pltpu.roll(x, LANES - LANES // 4, 1)
        before = pltpu.roll(x, LANES // 4, 1)
        high, low = split2(jnp.concatenate([x, jnp.where(is_re, after, -before)], axis=0))
        left.append(
            jnp.concatenate(
                [
                    jnp.concatenate([high, high], axis=1),
                    jnp.concatenate([low, jnp.zeros_like(low)], axis=1),
                ],
                axis=0,
            )
        )

    scale = 1.0 / FREQ_BINS

    def term(pair, g):
        return dot_rows(left[pair], right[pair, pl.ds(g * GROUP, GROUP)].reshape(GROUP * rows, 2 * LANES))

    def finished(acc):
        return ((acc[: 2 * rows] + acc[2 * rows :]) * scale).astype(out_ref.dtype)

    def take(pair, k, peer):
        piece(peer, peer, k, pair).wait_recv()
        right[pair, peer] = jnp.concatenate(split2(restored(blocks[pair, peer])), axis=1)

    def take_pair(pair):
        for_each_peer(chans, me, functools.partial(take, pair), (1, 2, 3, 4, 5, 6, 7))

    if chans == GROUP:
        acc = None
        for pair in range(pairs):
            take_pair(pair)
            acc = term(pair, 0) if acc is None else acc + term(pair, 0)
        out = finished(acc)
        out_ref[0, 0] = out[:rows]
        out_ref[0, 1] = out[rows:]
    else:
        for pair in range(pairs):
            take_pair(pair)

        @pl.loop(0, chans // GROUP)
        def _(g):
            out = finished(sum(term(pair, g) for pair in range(pairs)))
            at = pl.ds(pl.multiple_of(g * (GROUP * rows), LANES), GROUP * rows)
            out_ref[0, 0, :, at] = out[:rows]
            out_ref[0, 1, :, at] = out[rows:]

    for copy in halos + list(to_band.values()):
        copy.wait_send()
    for pair in range(pairs):
        for_each_peer(chans, me, lambda k, peer: piece(me, peer, k, pair).wait_send())


def body(chans, wins, strain, seg_ids, dead, radius):
    rows, windows, samples = strain.shape
    table = jnp.asarray(fourier_table(wins))
    width = 2 * FREQ_BINS
    dma = pltpu.SemaphoreType.DMA
    hbm = pl.BlockSpec(memory_space=pltpu.HBM)
    i32, i16 = jnp.int32, jnp.int16
    return pl.pallas_call(
        functools.partial(kernel, chans, wins),
        out_shape=pltpu.VMEM((1, 2, rows, chans * rows), BF16),
        in_specs=[hbm] * 5,
        out_specs=pl.BlockSpec(memory_space=pltpu.VMEM),
        scratch_shapes=[
            pltpu.VMEM((rows, samples), BF16),
            pltpu.VMEM(seg_ids.shape, i32),
            pltpu.VMEM((1, dead.shape[0]), i32),
            pltpu.VMEM((1, rows), i32),
            pltpu.VMEM(table.shape, F32),
            pltpu.VMEM((2, MOST_REACH, width), F32),
            pltpu.VMEM((2, MOST_REACH, width), F32),
            pltpu.VMEM((wins // 2, chans, rows, LANES), i16),
            pltpu.VMEM((2, wins, rows, LANES), i16),
            pltpu.VMEM((wins, rows, LANES), i16),
            pltpu.VMEM((wins // 2, chans, rows, 2 * LANES), BF16),
            dma((4,)),
            dma((TABLE_CUTS,)),
            dma((2,)),
            dma((2,)),
            dma((wins,)),
            dma((wins,)),
            dma((wins // 2, chans)),
            dma((wins // 2, chans)),
        ],
        compiler_params=pltpu.CompilerParams(
            collective_id=0, has_side_effects=True, vmem_limit_bytes=(63 if chans == GROUP else 48) * 2**20
        ),
    )(
        strain.reshape(rows * windows, samples),
        seg_ids,
        dead.reshape(1, -1),
        radius.reshape(1, -1),
        table,
    )


def solution(mesh):
    return jax.shard_map(
        functools.partial(body, mesh.shape["chan"], mesh.shape["win"]),
        mesh=mesh,
        in_specs=(P("chan", "win", None), P(), P(), P("chan")),
        out_specs=P("win", None, "chan", None),
        check_vma=False,
    )
```

```python
import functools
import math

import jax
import jax.numpy as jnp
import numpy as np
from jax import lax
from jax.experimental import pallas as pl
from jax.experimental.pallas import tpu as pltpu
from jax.sharding import PartitionSpec as P

SAMPLES = 1024
FREQ_BINS = 128
FIRST_BIN = 8
SMOOTH_BINS = 4
MOST_REACH = 8
FLOOR_POWER = 0.01
LANES = 128
TABLE_CUTS = 2
GROUP = 8
PEAK = 3.0
TOP_CODE = 32767.0
ROOT_SCALE = math.log2(TOP_CODE) - math.log2(PEAK) / 8.0

MESH = pl.DeviceIdType.MESH
F32 = jnp.float32
BF16 = jnp.bfloat16


def fourier_table(bands):
    band_bins = FREQ_BINS // bands
    half = SAMPLES // 2
    t = np.arange(half, dtype=np.int64)
    bins = FIRST_BIN + np.arange(FREQ_BINS, dtype=np.int64)
    angles = np.pi / SAMPLES * ((2 * t[:, None] + 1) * bins[None, :] % (2 * SAMPLES))
    taper = 0.5 - 0.5 * np.cos(2.0 * np.pi / SAMPLES * (t + 0.5))
    weights = taper[:, None] / np.sqrt(float(SAMPLES))
    cos, sin = weights * np.cos(angles), -weights * np.sin(angles)
    both = np.stack(
        [cos.reshape(half, bands, band_bins), sin.reshape(half, bands, band_bins)], axis=2
    ).reshape(half, 2 * FREQ_BINS)
    return both.astype(np.float32).reshape(TABLE_CUTS, half // TABLE_CUTS, -1)


def split3(x):
    high = x.astype(BF16)
    rest = x - high.astype(F32)
    middle = rest.astype(BF16)
    low = (rest - middle.astype(F32)).astype(BF16)
    return high, middle, low


def column_of(row, length, shift=0):
    shape = (length, row.shape[1])
    hit = lax.broadcasted_iota(jnp.int32, shape, 1) == lax.broadcasted_iota(jnp.int32, shape, 0) + shift
    return jnp.sum(jnp.where(hit, row, 0), axis=1, keepdims=True)


def links(seg, dead, radius, me, rows):
    channels, segments = seg.shape[1], dead.shape[1]
    start = me * rows - MOST_REACH
    turned = pltpu.roll(jnp.broadcast_to(seg, (8, channels)), lax.rem(channels - start, channels), 1)
    near = turned[0:1, 0:LANES]
    lane = lax.broadcasted_iota(jnp.int32, (1, LANES), 1)
    inside = (lane + start >= 0) & (lane + start < channels)
    dead_column = column_of(dead, segments)
    is_segment = lax.broadcasted_iota(jnp.int32, (segments, LANES), 0) == near
    dead_near = jnp.sum(jnp.where(is_segment, dead_column, 0), axis=0, keepdims=True)
    alive_near = jnp.where(inside, 1 - dead_near, 0)
    own_segs = column_of(near, rows, MOST_REACH)
    alive_own = column_of(alive_near, rows, MOST_REACH).astype(F32)
    reach = column_of(radius, rows)
    shape = (rows, LANES)
    offsets = lax.broadcasted_iota(jnp.int32, shape, 1) - lax.broadcasted_iota(jnp.int32, shape, 0) - MOST_REACH
    linked = (jnp.abs(offsets) <= reach) & (near == own_segs) & (alive_near > 0)
    linked = jnp.where(linked, 1.0, 0.0)
    counts = jnp.maximum(jnp.sum(linked, axis=1, keepdims=True), 1.0)
    lane = lax.broadcasted_iota(jnp.int32, shape, 1)
    own_first = pltpu.roll(linked, LANES - MOST_REACH, 1)
    linked = jnp.where(lane < rows, own_first, jnp.where(lane < rows + MOST_REACH, pltpu.roll(linked, rows, 1), linked))
    return linked[:, : rows + 2 * MOST_REACH].astype(BF16), alive_own, 1.0 / counts


def bin_of(lanes, bands):
    half = FREQ_BINS // bands
    return lanes // (2 * half) * half + lanes % half


def smoothing(bands):
    lanes = 2 * FREQ_BINS
    bins = bin_of(lax.broadcasted_iota(jnp.int32, (1, lanes), 1), bands)
    apart = bin_of(lax.broadcasted_iota(jnp.int32, (lanes, 1), 0), bands) - bins
    nearby = jnp.where(jnp.abs(apart) <= SMOOTH_BINS, 1.0, 0.0).astype(BF16)
    members = jnp.minimum(bins + SMOOTH_BINS, FREQ_BINS - 1) - jnp.maximum(bins - SMOOTH_BINS, 0) + 1
    return nearby, 1.0 / members.astype(F32)


def dot(a, b):
    return jnp.dot(a, b, preferred_element_type=F32)


def dot_rows(a, b):
    return lax.dot_general(a, b, (((1,), (1,)), ((), ())), preferred_element_type=F32)


def quantized(x, power, mean_power):
    root = jnp.exp2((jnp.log2(power) - jnp.log2(mean_power)) * 0.0625 + ROOT_SCALE)
    code = jnp.minimum(root + 0.5, TOP_CODE).astype(jnp.int32)
    return jnp.where(x < 0, -code, code)


def restored(codes):
    y = codes.astype(jnp.int32).astype(F32) * (1.0 / TOP_CODE)
    y2 = y * y
    y4 = y2 * y2
    size = (y4 * y4) * PEAK
    return jnp.where(y < 0, -size, size)


def split2(x):
    high = x.astype(BF16)
    return high, (x - high.astype(F32)).astype(BF16)


def for_each_peer(chans, me, act, order=(6, 7, 4, 5, 2, 3, 1)):
    if chans == GROUP:
        bits = [lax.rem(me // 2**i, 2) for i in range(3)]
        for k in order:
            act(k, me + sum((1 - 2 * bits[i]) * 2**i for i in range(3) if k >> i & 1))
    else:

        def step(k, carry):
            act(k, lax.rem(me + k, chans))
            return carry

        lax.fori_loop(1, chans, step, 0)


def kernel(
    chans, wins, strain_hbm, seg_hbm, dead_hbm, radius_hbm, table_hbm, out_ref,
    strain, seg, dead, radius, table, edges, halo_rows, blocks, chunks, arrived, right, load_sem, table_sem,
    halo_send, halo_recv, win_send, win_recv, pair_send, pair_recv,
):
    rows = strain_hbm.shape[0]
    width = 2 * FREQ_BINS
    me, win = lax.axis_index("chan"), lax.axis_index("win")

    barrier = pltpu.get_barrier_semaphore()

    def greet(k, peer):
        pl.semaphore_signal(barrier, inc=1, device_id={"chan": peer}, device_id_type=MESH)

    for_each_peer(chans, me, greet)
    for r in range(1, wins):
        pl.semaphore_signal(barrier, inc=1, device_id={"win": lax.rem(win + r, wins)}, device_id_type=MESH)

    loads = [
        pltpu.make_async_copy(src, dst, load_sem.at[i])
        for i, (src, dst) in enumerate(
            [(strain_hbm, strain), (seg_hbm, seg), (dead_hbm, dead), (radius_hbm, radius)]
        )
    ]
    table_loads = [
        pltpu.make_async_copy(table_hbm.at[i], table.at[i], table_sem.at[i]) for i in range(TABLE_CUTS)
    ]
    for load in loads + table_loads:
        load.start()

    nearby, per_member = smoothing(wins)
    for load in loads:
        load.wait()
    linked, alive, per_count = links(seg[...].reshape(1, -1), dead[...], radius[...], me, rows)

    cut = SAMPLES // 2 // TABLE_CUTS
    shape = (cut, cut)
    flips = lax.broadcasted_iota(jnp.int32, shape, 0) + lax.broadcasted_iota(jnp.int32, shape, 1) == cut - 1
    last_cuts = [strain[:, SAMPLES - (i + 1) * cut : SAMPLES - i * cut] for i in range(TABLE_CUTS)]
    backwards = dot(jnp.concatenate(last_cuts, axis=0), jnp.where(flips, 1.0, 0.0).astype(BF16)).astype(BF16)
    total = None
    for i in range(TABLE_CUTS):
        samples = jnp.concatenate(
            [strain[:, i * cut : (i + 1) * cut], backwards[i * rows : (i + 1) * rows]], axis=0
        )
        table_loads[i].wait()
        term = dot(samples, jnp.concatenate(split3(table[i]), axis=1))
        total = term if total is None else total + term
    total = total[:, :width] + total[:, width : 2 * width] + total[:, 2 * width :]
    is_cos = lax.broadcasted_iota(jnp.int32, (1, width), 1) % (width // wins) < width // wins // 2
    own = total[:rows] + jnp.where(is_cos, 1.0, -1.0) * total[rows:]
    edges[0] = own[rows - MOST_REACH :]
    edges[1] = own[:MOST_REACH]
    own_parts = jnp.concatenate(split3(own), axis=1)

    pl.semaphore_wait(barrier, chans - 1 + wins - 1)

    halos = [
        pltpu.make_async_remote_copy(
            src_ref=edges.at[side],
            dst_ref=halo_rows.at[side],
            send_sem=halo_send.at[side],
            recv_sem=halo_recv.at[side],
            device_id={"chan": lax.rem(me + step, chans)},
            device_id_type=MESH,
        )
        for side, step in enumerate((1, chans - 1))
    ]
    for halo in halos:
        halo.start()
    for halo in halos:
        halo.wait_recv()

    near_rows = halo_rows[...].reshape(2 * MOST_REACH, width)
    near_parts = jnp.concatenate(split3(near_rows), axis=1)
    sums = dot(linked, jnp.concatenate([own_parts, near_parts], axis=0))
    sums = sums[:, :width] + sums[:, width : 2 * width] + sums[:, 2 * width :]
    spectra = alive * (own - sums * per_count)
    power = spectra * spectra
    smooth = dot(jnp.concatenate(split2(power), axis=0), nearby)
    smooth = (smooth[:rows] + smooth[rows:]) * per_member
    codes = quantized(spectra, power, jnp.maximum(smooth, FLOOR_POWER))

    for j in range(wins // 2):
        tile = codes[:, j * LANES : (j + 1) * LANES]
        turned = pltpu.roll(tile, LANES // 2, 1).astype(jnp.int16)
        tile = tile.astype(jnp.int16)
        for h in range(2):
            chunks[h, 2 * j + h] = tile
            chunks[h, 2 * j + 1 - h] = turned

    to_band = {}
    for r in range(wins - 1, 0, -1):
        band = win + sum((1 - 2 * lax.rem(win // 2**i, 2)) * 2**i for i in range(2) if r >> i & 1)
        copy = pltpu.make_async_remote_copy(
            src_ref=chunks.at[r % 2, band],
            dst_ref=arrived.at[r],
            send_sem=win_send.at[r],
            recv_sem=win_recv.at[r],
            device_id={"win": band},
            device_id_type=MESH,
        )
        copy.start()
        to_band[r] = copy

    def piece(owner, peer, k, pair):
        return pltpu.make_async_remote_copy(
            src_ref=blocks.at[pair, owner],
            dst_ref=blocks.at[pair, owner],
            send_sem=pair_send.at[pair, k],
            recv_sem=pair_recv.at[pair, owner],
            device_id={"chan": peer},
            device_id_type=MESH,
        )

    in_first = lax.broadcasted_iota(jnp.int32, (rows, LANES), 1) < LANES // 2
    is_re = lax.broadcasted_iota(jnp.int32, (rows, LANES), 1) % (LANES // 2) < LANES // 4
    pairs = wins // 2
    left = []
    for pair in range(pairs):
        if pair > 0:
            to_band[2 * pair].wait_recv()
        to_band[2 * pair + 1].wait_recv()
        even = chunks[0, win] if pair == 0 else arrived[2 * pair]
        both = jnp.where(in_first, even.astype(jnp.int32), arrived[2 * pair + 1].astype(jnp.int32))
        blocks[pair, me] = both.astype(jnp.int16)
        for_each_peer(chans, me, lambda k, peer: piece(me, peer, k, pair).start())
        x = restored(both)
        right[pair, me] = jnp.concatenate(split2(x), axis=1)
        after = pltpu.roll(x, LANES - LANES // 4, 1)
        before = pltpu.roll(x, LANES // 4, 1)
        high, low = split2(jnp.concatenate([x, jnp.where(is_re, after, -before)], axis=0))
        left.append(
            jnp.concatenate(
                [
                    jnp.concatenate([high, high], axis=1),
                    jnp.concatenate([low, jnp.zeros_like(low)], axis=1),
                ],
                axis=0,
            )
        )

    scale = 1.0 / FREQ_BINS

    def term(pair, g):
        return dot_rows(left[pair], right[pair, pl.ds(g * GROUP, GROUP)].reshape(GROUP * rows, 2 * LANES))

    def finished(acc):
        return ((acc[: 2 * rows] + acc[2 * rows :]) * scale).astype(out_ref.dtype)

    def take(pair, k, peer):
        piece(peer, peer, k, pair).wait_recv()
        right[pair, peer] = jnp.concatenate(split2(restored(blocks[pair, peer])), axis=1)

    def take_pair(pair):
        for_each_peer(chans, me, functools.partial(take, pair), (1, 2, 3, 4, 5, 6, 7))

    if chans == GROUP:
        acc = None
        for pair in range(pairs):
            take_pair(pair)
            acc = term(pair, 0) if acc is None else acc + term(pair, 0)
        out = finished(acc)
        out_ref[0, 0] = out[:rows]
        out_ref[0, 1] = out[rows:]
    else:
        for pair in range(pairs):
            take_pair(pair)

        @pl.loop(0, chans // GROUP)
        def _(g):
            out = finished(sum(term(pair, g) for pair in range(pairs)))
            at = pl.ds(pl.multiple_of(g * (GROUP * rows), LANES), GROUP * rows)
            out_ref[0, 0, :, at] = out[:rows]
            out_ref[0, 1, :, at] = out[rows:]

    for copy in halos + list(to_band.values()):
        copy.wait_send()
    for pair in range(pairs):
        for_each_peer(chans, me, lambda k, peer: piece(me, peer, k, pair).wait_send())


def body(chans, wins, strain, seg_ids, dead, radius):
    rows, windows, samples = strain.shape
    table = jnp.asarray(fourier_table(wins))
    width = 2 * FREQ_BINS
    dma = pltpu.SemaphoreType.DMA
    hbm = pl.BlockSpec(memory_space=pltpu.HBM)
    i32, i16 = jnp.int32, jnp.int16
    return pl.pallas_call(
        functools.partial(kernel, chans, wins),
        out_shape=pltpu.VMEM((1, 2, rows, chans * rows), BF16),
        in_specs=[hbm] * 5,
        out_specs=pl.BlockSpec(memory_space=pltpu.VMEM),
        scratch_shapes=[
            pltpu.VMEM((rows, samples), BF16),
            pltpu.VMEM(seg_ids.shape, i32),
            pltpu.VMEM((1, dead.shape[0]), i32),
            pltpu.VMEM((1, rows), i32),
            pltpu.VMEM(table.shape, F32),
            pltpu.VMEM((2, MOST_REACH, width), F32),
            pltpu.VMEM((2, MOST_REACH, width), F32),
            pltpu.VMEM((wins // 2, chans, rows, LANES), i16),
            pltpu.VMEM((2, wins, rows, LANES), i16),
            pltpu.VMEM((wins, rows, LANES), i16),
            pltpu.VMEM((wins // 2, chans, rows, 2 * LANES), BF16),
            dma((4,)),
            dma((TABLE_CUTS,)),
            dma((2,)),
            dma((2,)),
            dma((wins,)),
            dma((wins,)),
            dma((wins // 2, chans)),
            dma((wins // 2, chans)),
        ],
        compiler_params=pltpu.CompilerParams(
            collective_id=0, has_side_effects=True, vmem_limit_bytes=(63 if chans == GROUP else 48) * 2**20
        ),
    )(
        strain.reshape(rows * windows, samples),
        seg_ids,
        dead.reshape(1, -1),
        radius.reshape(1, -1),
        table,
    )


def solution(mesh):
    return jax.shard_map(
        functools.partial(body, mesh.shape["chan"], mesh.shape["win"]),
        mesh=mesh,
        in_specs=(P("chan", "win", None), P(), P(), P("chan")),
        out_specs=P("win", None, "chan", None),
        check_vma=False,
    )
```

```python
import functools
import math

import jax
import jax.numpy as jnp
import numpy as np
from jax import lax
from jax.experimental import pallas as pl
from jax.experimental.pallas import tpu as pltpu
from jax.sharding import PartitionSpec as P

SAMPLES = 1024
FREQ_BINS = 128
FIRST_BIN = 8
SMOOTH_BINS = 4
MOST_REACH = 8
FLOOR_POWER = 0.01
LANES = 128
TABLE_CUTS = 2
GROUP = 8
DIRECT = (6, 4, 2, 1)
PEAK = 3.0
TOP_CODE = 32767.0
ROOT_SCALE = math.log2(TOP_CODE) - math.log2(PEAK) / 8.0

MESH = pl.DeviceIdType.MESH
F32 = jnp.float32
BF16 = jnp.bfloat16


def fourier_table(bands):
    band_bins = FREQ_BINS // bands
    half = SAMPLES // 2
    t = np.arange(half, dtype=np.int64)
    bins = FIRST_BIN + np.arange(FREQ_BINS, dtype=np.int64)
    angles = np.pi / SAMPLES * ((2 * t[:, None] + 1) * bins[None, :] % (2 * SAMPLES))
    taper = 0.5 - 0.5 * np.cos(2.0 * np.pi / SAMPLES * (t + 0.5))
    weights = taper[:, None] / np.sqrt(float(SAMPLES))
    cos, sin = weights * np.cos(angles), -weights * np.sin(angles)
    both = np.stack(
        [cos.reshape(half, bands, band_bins), sin.reshape(half, bands, band_bins)], axis=2
    ).reshape(half, 2 * FREQ_BINS)
    return both.astype(np.float32).reshape(TABLE_CUTS, half // TABLE_CUTS, -1)


def split3(x):
    high = x.astype(BF16)
    rest = x - high.astype(F32)
    middle = rest.astype(BF16)
    low = (rest - middle.astype(F32)).astype(BF16)
    return high, middle, low


def column_of(row, length, shift=0):
    shape = (length, row.shape[1])
    hit = lax.broadcasted_iota(jnp.int32, shape, 1) == lax.broadcasted_iota(jnp.int32, shape, 0) + shift
    return jnp.sum(jnp.where(hit, row, 0), axis=1, keepdims=True)


def links(seg, dead, radius, me, rows):
    channels, segments = seg.shape[1], dead.shape[1]
    start = me * rows - MOST_REACH
    turned = pltpu.roll(jnp.broadcast_to(seg, (8, channels)), lax.rem(channels - start, channels), 1)
    near = turned[0:1, 0:LANES]
    lane = lax.broadcasted_iota(jnp.int32, (1, LANES), 1)
    inside = (lane + start >= 0) & (lane + start < channels)
    dead_column = column_of(dead, segments)
    is_segment = lax.broadcasted_iota(jnp.int32, (segments, LANES), 0) == near
    dead_near = jnp.sum(jnp.where(is_segment, dead_column, 0), axis=0, keepdims=True)
    alive_near = jnp.where(inside, 1 - dead_near, 0)
    own_segs = column_of(near, rows, MOST_REACH)
    alive_own = column_of(alive_near, rows, MOST_REACH).astype(F32)
    reach = column_of(radius, rows)
    shape = (rows, LANES)
    offsets = lax.broadcasted_iota(jnp.int32, shape, 1) - lax.broadcasted_iota(jnp.int32, shape, 0) - MOST_REACH
    linked = (jnp.abs(offsets) <= reach) & (near == own_segs) & (alive_near > 0)
    linked = jnp.where(linked, 1.0, 0.0)
    counts = jnp.maximum(jnp.sum(linked, axis=1, keepdims=True), 1.0)
    lane = lax.broadcasted_iota(jnp.int32, shape, 1)
    own_first = pltpu.roll(linked, LANES - MOST_REACH, 1)
    linked = jnp.where(lane < rows, own_first, jnp.where(lane < rows + MOST_REACH, pltpu.roll(linked, rows, 1), linked))
    return linked[:, : rows + 2 * MOST_REACH].astype(BF16), alive_own, 1.0 / counts


def bin_of(lanes, bands):
    half = FREQ_BINS // bands
    return lanes // (2 * half) * half + lanes % half


def smoothing(bands):
    lanes = 2 * FREQ_BINS
    bins = bin_of(lax.broadcasted_iota(jnp.int32, (1, lanes), 1), bands)
    apart = bin_of(lax.broadcasted_iota(jnp.int32, (lanes, 1), 0), bands) - bins
    nearby = jnp.where(jnp.abs(apart) <= SMOOTH_BINS, 1.0, 0.0).astype(BF16)
    members = jnp.minimum(bins + SMOOTH_BINS, FREQ_BINS - 1) - jnp.maximum(bins - SMOOTH_BINS, 0) + 1
    return nearby, 1.0 / members.astype(F32)


def dot(a, b):
    return jnp.dot(a, b, preferred_element_type=F32)


def dot_rows(a, b):
    return lax.dot_general(a, b, (((1,), (1,)), ((), ())), preferred_element_type=F32)


def quantized(x, power, mean_power):
    root = jnp.exp2((jnp.log2(power) - jnp.log2(mean_power)) * 0.0625 + ROOT_SCALE)
    code = jnp.minimum(root + 0.5, TOP_CODE).astype(jnp.int32)
    return jnp.where(x < 0, -code, code)


def restored(codes):
    y = codes.astype(jnp.int32).astype(F32) * (1.0 / TOP_CODE)
    y2 = y * y
    y4 = y2 * y2
    size = (y4 * y4) * PEAK
    return jnp.where(y < 0, -size, size)


def split2(x):
    high = x.astype(BF16)
    return high, (x - high.astype(F32)).astype(BF16)


def block_at(me, distance):
    return me + sum((1 - 2 * lax.rem(me // 2**i, 2)) * 2**i for i in range(3) if distance >> i & 1)


def for_each_peer(chans, me, act, order):
    if chans == GROUP:
        for k in order:
            act(k, block_at(me, k))
    else:

        def step(k, carry):
            act(k, lax.rem(me + k, chans))
            return carry

        lax.fori_loop(1, chans, step, 0)


def kernel(
    chans, wins, strain_hbm, seg_hbm, dead_hbm, radius_hbm, table_hbm, out_ref,
    strain, seg, dead, radius, table, edges, halo_rows, blocks, chunks, arrived, right, load_sem, table_sem,
    halo_send, halo_recv, win_send, win_recv, pair_send, pair_recv,
):
    rows = strain_hbm.shape[0]
    width = 2 * FREQ_BINS
    me, win = lax.axis_index("chan"), lax.axis_index("win")

    barrier = pltpu.get_barrier_semaphore()

    def greet(k, peer):
        pl.semaphore_signal(barrier, inc=1, device_id={"chan": peer}, device_id_type=MESH)

    for_each_peer(chans, me, greet, DIRECT)
    greeted = chans - 1
    if chans == GROUP:
        greet(0, lax.rem(me + chans + 2 * lax.rem(me, 2) - 1, chans))
        greeted = len(DIRECT) + 1
    for r in range(1, wins):
        pl.semaphore_signal(barrier, inc=1, device_id={"win": lax.rem(win + r, wins)}, device_id_type=MESH)

    loads = [
        pltpu.make_async_copy(src, dst, load_sem.at[i])
        for i, (src, dst) in enumerate(
            [(strain_hbm, strain), (seg_hbm, seg), (dead_hbm, dead), (radius_hbm, radius)]
        )
    ]
    table_loads = [
        pltpu.make_async_copy(table_hbm.at[i], table.at[i], table_sem.at[i]) for i in range(TABLE_CUTS)
    ]
    for load in loads + table_loads:
        load.start()

    nearby, per_member = smoothing(wins)
    for load in loads:
        load.wait()
    linked, alive, per_count = links(seg[...].reshape(1, -1), dead[...], radius[...], me, rows)

    cut = SAMPLES // 2 // TABLE_CUTS
    shape = (cut, cut)
    flips = lax.broadcasted_iota(jnp.int32, shape, 0) + lax.broadcasted_iota(jnp.int32, shape, 1) == cut - 1
    last_cuts = [strain[:, SAMPLES - (i + 1) * cut : SAMPLES - i * cut] for i in range(TABLE_CUTS)]
    backwards = dot(jnp.concatenate(last_cuts, axis=0), jnp.where(flips, 1.0, 0.0).astype(BF16)).astype(BF16)
    total = None
    for i in range(TABLE_CUTS):
        samples = jnp.concatenate(
            [strain[:, i * cut : (i + 1) * cut], backwards[i * rows : (i + 1) * rows]], axis=0
        )
        table_loads[i].wait()
        term = dot(samples, jnp.concatenate(split3(table[i]), axis=1))
        total = term if total is None else total + term
    total = total[:, :width] + total[:, width : 2 * width] + total[:, 2 * width :]
    is_cos = lax.broadcasted_iota(jnp.int32, (1, width), 1) % (width // wins) < width // wins // 2
    own = total[:rows] + jnp.where(is_cos, 1.0, -1.0) * total[rows:]
    edges[0] = own[rows - MOST_REACH :]
    edges[1] = own[:MOST_REACH]
    own_parts = jnp.concatenate(split3(own), axis=1)

    pl.semaphore_wait(barrier, greeted + wins - 1)

    halos = [
        pltpu.make_async_remote_copy(
            src_ref=edges.at[side],
            dst_ref=halo_rows.at[side],
            send_sem=halo_send.at[side],
            recv_sem=halo_recv.at[side],
            device_id={"chan": lax.rem(me + step, chans)},
            device_id_type=MESH,
        )
        for side, step in enumerate((1, chans - 1))
    ]
    for halo in halos:
        halo.start()
    for halo in halos:
        halo.wait_recv()

    near_rows = halo_rows[...].reshape(2 * MOST_REACH, width)
    near_parts = jnp.concatenate(split3(near_rows), axis=1)
    sums = dot(linked, jnp.concatenate([own_parts, near_parts], axis=0))
    sums = sums[:, :width] + sums[:, width : 2 * width] + sums[:, 2 * width :]
    spectra = alive * (own - sums * per_count)
    power = spectra * spectra
    smooth = dot(jnp.concatenate(split2(power), axis=0), nearby)
    smooth = (smooth[:rows] + smooth[rows:]) * per_member
    codes = quantized(spectra, power, jnp.maximum(smooth, FLOOR_POWER))

    for j in range(wins // 2):
        tile = codes[:, j * LANES : (j + 1) * LANES]
        turned = pltpu.roll(tile, LANES // 2, 1).astype(jnp.int16)
        tile = tile.astype(jnp.int16)
        for h in range(2):
            chunks[h, 2 * j + h] = tile
            chunks[h, 2 * j + 1 - h] = turned

    to_band = {}
    for r in range(wins - 1, 0, -1):
        band = win + sum((1 - 2 * lax.rem(win // 2**i, 2)) * 2**i for i in range(2) if r >> i & 1)
        copy = pltpu.make_async_remote_copy(
            src_ref=chunks.at[r % 2, band],
            dst_ref=arrived.at[r],
            send_sem=win_send.at[r],
            recv_sem=win_recv.at[r],
            device_id={"win": band},
            device_id_type=MESH,
        )
        copy.start()
        to_band[r] = copy

    def piece(owner, peer, pair, passed=0):
        return pltpu.make_async_remote_copy(
            src_ref=blocks.at[pair, owner],
            dst_ref=blocks.at[pair, owner],
            send_sem=pair_send.at[pair, passed],
            recv_sem=pair_recv.at[pair, owner],
            device_id={"chan": peer},
            device_id_type=MESH,
        )

    in_first = lax.broadcasted_iota(jnp.int32, (rows, LANES), 1) < LANES // 2
    is_re = lax.broadcasted_iota(jnp.int32, (rows, LANES), 1) % (LANES // 2) < LANES // 4
    pairs = wins // 2
    left = []
    for pair in range(pairs):
        if pair > 0:
            to_band[2 * pair].wait_recv()
        to_band[2 * pair + 1].wait_recv()
        even = chunks[0, win] if pair == 0 else arrived[2 * pair]
        both = jnp.where(in_first, even.astype(jnp.int32), arrived[2 * pair + 1].astype(jnp.int32))
        blocks[pair, me] = both.astype(jnp.int16)
        for_each_peer(chans, me, lambda k, peer: piece(me, peer, pair).start(), DIRECT)
        x = restored(both)
        right[pair, me] = jnp.concatenate(split2(x), axis=1)
        after = pltpu.roll(x, LANES - LANES // 4, 1)
        before = pltpu.roll(x, LANES // 4, 1)
        high, low = split2(jnp.concatenate([x, jnp.where(is_re, after, -before)], axis=0))
        left.append(
            jnp.concatenate(
                [
                    jnp.concatenate([high, high], axis=1),
                    jnp.concatenate([low, jnp.zeros_like(low)], axis=1),
                ],
                axis=0,
            )
        )

    scale = 1.0 / FREQ_BINS

    def term(pair, g):
        return dot_rows(left[pair], right[pair, pl.ds(g * GROUP, GROUP)].reshape(GROUP * rows, 2 * LANES))

    def finished(acc):
        return ((acc[: 2 * rows] + acc[2 * rows :]) * scale).astype(out_ref.dtype)

    def arrive(pair, k, owner):
        piece(owner, owner, pair).wait_recv()

    def decode(pair, k, owner):
        right[pair, owner] = jnp.concatenate(split2(restored(blocks[pair, owner])), axis=1)

    def take(pair, k, owner):
        arrive(pair, k, owner)
        decode(pair, k, owner)

    def take_pair(pair):
        if chans == GROUP:
            for k in (2, 4, 6):
                owner = block_at(me, k)
                arrive(pair, k, owner)
                piece(owner, block_at(me, 1), pair, 1).start()
            for k in (2, 4, 6):
                decode(pair, k, block_at(me, k))
            for k in (1, 3, 5, 7):
                take(pair, k, block_at(me, k))
        else:
            for_each_peer(chans, me, functools.partial(take, pair), ())

    if chans == GROUP:
        acc = None
        for pair in range(pairs):
            take_pair(pair)
            acc = term(pair, 0) if acc is None else acc + term(pair, 0)
        out = finished(acc)
        out_ref[0, 0] = out[:rows]
        out_ref[0, 1] = out[rows:]
    else:
        for pair in range(pairs):
            take_pair(pair)

        @pl.loop(0, chans // GROUP)
        def _(g):
            out = finished(sum(term(pair, g) for pair in range(pairs)))
            at = pl.ds(pl.multiple_of(g * (GROUP * rows), LANES), GROUP * rows)
            out_ref[0, 0, :, at] = out[:rows]
            out_ref[0, 1, :, at] = out[rows:]

    for copy in halos + list(to_band.values()):
        copy.wait_send()
    for pair in range(pairs):
        for passed, count in enumerate((4, 3) if chans == GROUP else (chans - 1,)):
            sent = blocks.at[pair, pl.ds(0, count)]
            pltpu.make_async_remote_copy(
                src_ref=sent,
                dst_ref=sent,
                send_sem=pair_send.at[pair, passed],
                recv_sem=pair_recv.at[pair, me],
                device_id={"chan": lax.rem(me + 1, chans)},
                device_id_type=MESH,
            ).wait_send()


def body(chans, wins, strain, seg_ids, dead, radius):
    rows, windows, samples = strain.shape
    table = jnp.asarray(fourier_table(wins))
    width = 2 * FREQ_BINS
    dma = pltpu.SemaphoreType.DMA
    hbm = pl.BlockSpec(memory_space=pltpu.HBM)
    i32, i16 = jnp.int32, jnp.int16
    return pl.pallas_call(
        functools.partial(kernel, chans, wins),
        out_shape=pltpu.VMEM((1, 2, rows, chans * rows), BF16),
        in_specs=[hbm] * 5,
        out_specs=pl.BlockSpec(memory_space=pltpu.VMEM),
        scratch_shapes=[
            pltpu.VMEM((rows, samples), BF16),
            pltpu.VMEM(seg_ids.shape, i32),
            pltpu.VMEM((1, dead.shape[0]), i32),
            pltpu.VMEM((1, rows), i32),
            pltpu.VMEM(table.shape, F32),
            pltpu.VMEM((2, MOST_REACH, width), F32),
            pltpu.VMEM((2, MOST_REACH, width), F32),
            pltpu.VMEM((wins // 2, chans, rows, LANES), i16),
            pltpu.VMEM((2, wins, rows, LANES), i16),
            pltpu.VMEM((wins, rows, LANES), i16),
            pltpu.VMEM((wins // 2, chans, rows, 2 * LANES), BF16),
            dma((4,)),
            dma((TABLE_CUTS,)),
            dma((2,)),
            dma((2,)),
            dma((wins,)),
            dma((wins,)),
            dma((wins // 2, 2)),
            dma((wins // 2, chans)),
        ],
        compiler_params=pltpu.CompilerParams(
            collective_id=0, has_side_effects=True, vmem_limit_bytes=(63 if chans == GROUP else 48) * 2**20
        ),
    )(
        strain.reshape(rows * windows, samples),
        seg_ids,
        dead.reshape(1, -1),
        radius.reshape(1, -1),
        table,
    )


def solution(mesh):
    return jax.shard_map(
        functools.partial(body, mesh.shape["chan"], mesh.shape["win"]),
        mesh=mesh,
        in_specs=(P("chan", "win", None), P(), P(), P("chan")),
        out_specs=P("win", None, "chan", None),
        check_vma=False,
    )
```

```python
import functools
import math

import jax
import jax.numpy as jnp
import numpy as np
from jax import lax
from jax.experimental import pallas as pl
from jax.experimental.pallas import tpu as pltpu
from jax.sharding import PartitionSpec as P

SAMPLES = 1024
FREQ_BINS = 128
FIRST_BIN = 8
SMOOTH_BINS = 4
MOST_REACH = 8
FLOOR_POWER = 0.01
LANES = 128
TABLE_CUTS = 2
GROUP = 8
PEAK = 3.0
TOP_CODE = 32767.0
ROOT_SCALE = math.log2(TOP_CODE) - math.log2(PEAK) / 8.0

MESH = pl.DeviceIdType.MESH
F32 = jnp.float32
BF16 = jnp.bfloat16


def fourier_table(bands):
    band_bins = FREQ_BINS // bands
    half = SAMPLES // 2
    t = np.arange(half, dtype=np.int64)
    bins = FIRST_BIN + np.arange(FREQ_BINS, dtype=np.int64)
    angles = np.pi / SAMPLES * ((2 * t[:, None] + 1) * bins[None, :] % (2 * SAMPLES))
    taper = 0.5 - 0.5 * np.cos(2.0 * np.pi / SAMPLES * (t + 0.5))
    weights = taper[:, None] / np.sqrt(float(SAMPLES))
    cos, sin = weights * np.cos(angles), -weights * np.sin(angles)
    both = np.stack(
        [cos.reshape(half, bands, band_bins), sin.reshape(half, bands, band_bins)], axis=2
    ).reshape(half, 2 * FREQ_BINS)
    return both.astype(np.float32).reshape(TABLE_CUTS, half // TABLE_CUTS, -1)


def split3(x):
    high = x.astype(BF16)
    rest = x - high.astype(F32)
    middle = rest.astype(BF16)
    low = (rest - middle.astype(F32)).astype(BF16)
    return high, middle, low


def column_of(row, length, shift=0):
    shape = (length, row.shape[1])
    hit = lax.broadcasted_iota(jnp.int32, shape, 1) == lax.broadcasted_iota(jnp.int32, shape, 0) + shift
    return jnp.sum(jnp.where(hit, row, 0), axis=1, keepdims=True)


def links(seg, dead, radius, me, rows):
    channels, segments = seg.shape[1], dead.shape[1]
    start = me * rows - MOST_REACH
    turned = pltpu.roll(jnp.broadcast_to(seg, (8, channels)), lax.rem(channels - start, channels), 1)
    near = turned[0:1, 0:LANES]
    lane = lax.broadcasted_iota(jnp.int32, (1, LANES), 1)
    inside = (lane + start >= 0) & (lane + start < channels)
    dead_column = column_of(dead, segments)
    is_segment = lax.broadcasted_iota(jnp.int32, (segments, LANES), 0) == near
    dead_near = jnp.sum(jnp.where(is_segment, dead_column, 0), axis=0, keepdims=True)
    alive_near = jnp.where(inside, 1 - dead_near, 0)
    own_segs = column_of(near, rows, MOST_REACH)
    alive_own = column_of(alive_near, rows, MOST_REACH).astype(F32)
    reach = column_of(radius, rows)
    shape = (rows, LANES)
    offsets = lax.broadcasted_iota(jnp.int32, shape, 1) - lax.broadcasted_iota(jnp.int32, shape, 0) - MOST_REACH
    linked = (jnp.abs(offsets) <= reach) & (near == own_segs) & (alive_near > 0)
    linked = jnp.where(linked, 1.0, 0.0)
    counts = jnp.maximum(jnp.sum(linked, axis=1, keepdims=True), 1.0)
    lane = lax.broadcasted_iota(jnp.int32, shape, 1)
    own_first = pltpu.roll(linked, LANES - MOST_REACH, 1)
    linked = jnp.where(lane < rows, own_first, jnp.where(lane < rows + MOST_REACH, pltpu.roll(linked, rows, 1), linked))
    return linked[:, : rows + 2 * MOST_REACH].astype(BF16), alive_own, 1.0 / counts


def bin_of(lanes, bands):
    half = FREQ_BINS // bands
    return lanes // (2 * half) * half + lanes % half


def smoothing(bands):
    lanes = 2 * FREQ_BINS
    bins = bin_of(lax.broadcasted_iota(jnp.int32, (1, lanes), 1), bands)
    apart = bin_of(lax.broadcasted_iota(jnp.int32, (lanes, 1), 0), bands) - bins
    nearby = jnp.where(jnp.abs(apart) <= SMOOTH_BINS, 1.0, 0.0).astype(BF16)
    members = jnp.minimum(bins + SMOOTH_BINS, FREQ_BINS - 1) - jnp.maximum(bins - SMOOTH_BINS, 0) + 1
    return nearby, 1.0 / members.astype(F32)


def dot(a, b):
    return jnp.dot(a, b, preferred_element_type=F32)


def dot_rows(a, b):
    return lax.dot_general(a, b, (((1,), (1,)), ((), ())), preferred_element_type=F32)


def quantized(x, power, mean_power):
    root = jnp.exp2((jnp.log2(power) - jnp.log2(mean_power)) * 0.0625 + ROOT_SCALE)
    code = jnp.minimum(root + 0.5, TOP_CODE).astype(jnp.int32)
    return jnp.where(x < 0, -code, code)


def restored(codes):
    y = codes.astype(jnp.int32).astype(F32) * (1.0 / TOP_CODE)
    y2 = y * y
    y4 = y2 * y2
    size = (y4 * y4) * PEAK
    return jnp.where(y < 0, -size, size)


def split2(x):
    high = x.astype(BF16)
    return high, (x - high.astype(F32)).astype(BF16)


def for_each_peer(chans, me, act, order=(6, 7, 4, 5, 2, 3, 1)):
    if chans == GROUP:
        bits = [lax.rem(me // 2**i, 2) for i in range(3)]
        for k in order:
            act(k, me + sum((1 - 2 * bits[i]) * 2**i for i in range(3) if k >> i & 1))
    else:

        def step(k, carry):
            act(k, lax.rem(me + k, chans))
            return carry

        lax.fori_loop(1, chans, step, 0)


def kernel(
    chans, wins, strain_hbm, seg_hbm, dead_hbm, radius_hbm, table_hbm, out_ref,
    strain, seg, dead, radius, table, edges, halo_rows, blocks, chunks, arrived, right, load_sem, table_sem,
    halo_send, halo_recv, win_send, win_recv, pair_send, pair_recv,
):
    rows = strain_hbm.shape[0]
    width = 2 * FREQ_BINS
    me, win = lax.axis_index("chan"), lax.axis_index("win")

    strain_load = pltpu.make_async_copy(strain_hbm, strain, load_sem.at[0])
    table_loads = [
        pltpu.make_async_copy(table_hbm.at[i], table.at[i], table_sem.at[i]) for i in range(TABLE_CUTS)
    ]
    for load in [strain_load] + table_loads:
        load.start()

    barrier = pltpu.get_barrier_semaphore()

    def greet(k, peer):
        pl.semaphore_signal(barrier, inc=1, device_id={"chan": peer}, device_id_type=MESH)

    for_each_peer(chans, me, greet)
    for r in range(1, wins):
        pl.semaphore_signal(barrier, inc=1, device_id={"win": lax.rem(win + r, wins)}, device_id_type=MESH)

    loads = [
        pltpu.make_async_copy(src, dst, load_sem.at[1 + i])
        for i, (src, dst) in enumerate([(seg_hbm, seg), (dead_hbm, dead), (radius_hbm, radius)])
    ]
    for load in loads:
        load.start()

    nearby, per_member = smoothing(wins)
    for load in loads:
        load.wait()
    linked, alive, per_count = links(seg[...].reshape(1, -1), dead[...], radius[...], me, rows)

    strain_load.wait()
    cut = SAMPLES // 2 // TABLE_CUTS
    shape = (cut, cut)
    flips = lax.broadcasted_iota(jnp.int32, shape, 0) + lax.broadcasted_iota(jnp.int32, shape, 1) == cut - 1
    last_cuts = [strain[:, SAMPLES - (i + 1) * cut : SAMPLES - i * cut] for i in range(TABLE_CUTS)]
    backwards = dot(jnp.concatenate(last_cuts, axis=0), jnp.where(flips, 1.0, 0.0).astype(BF16)).astype(BF16)
    total = None
    for i in range(TABLE_CUTS):
        samples = jnp.concatenate(
            [strain[:, i * cut : (i + 1) * cut], backwards[i * rows : (i + 1) * rows]], axis=0
        )
        table_loads[i].wait()
        term = dot(samples, jnp.concatenate(split3(table[i]), axis=1))
        total = term if total is None else total + term
    total = total[:, :width] + total[:, width : 2 * width] + total[:, 2 * width :]
    is_cos = lax.broadcasted_iota(jnp.int32, (1, width), 1) % (width // wins) < width // wins // 2
    own = total[:rows] + jnp.where(is_cos, 1.0, -1.0) * total[rows:]
    edges[0] = own[rows - MOST_REACH :]
    edges[1] = own[:MOST_REACH]
    own_parts = jnp.concatenate(split3(own), axis=1)

    pl.semaphore_wait(barrier, chans - 1 + wins - 1)

    halos = [
        pltpu.make_async_remote_copy(
            src_ref=edges.at[side],
            dst_ref=halo_rows.at[side],
            send_sem=halo_send.at[side],
            recv_sem=halo_recv.at[side],
            device_id={"chan": lax.rem(me + step, chans)},
            device_id_type=MESH,
        )
        for side, step in enumerate((1, chans - 1))
    ]
    for halo in halos:
        halo.start()
    for halo in halos:
        halo.wait_recv()

    near_rows = halo_rows[...].reshape(2 * MOST_REACH, width)
    near_parts = jnp.concatenate(split3(near_rows), axis=1)
    sums = dot(linked, jnp.concatenate([own_parts, near_parts], axis=0))
    sums = sums[:, :width] + sums[:, width : 2 * width] + sums[:, 2 * width :]
    spectra = alive * (own - sums * per_count)
    power = spectra * spectra
    smooth = dot(jnp.concatenate(split2(power), axis=0), nearby)
    smooth = (smooth[:rows] + smooth[rows:]) * per_member
    codes = quantized(spectra, power, jnp.maximum(smooth, FLOOR_POWER))

    for j in range(wins // 2):
        tile = codes[:, j * LANES : (j + 1) * LANES]
        turned = pltpu.roll(tile, LANES // 2, 1).astype(jnp.int16)
        tile = tile.astype(jnp.int16)
        for h in range(2):
            chunks[h, 2 * j + h] = tile
            chunks[h, 2 * j + 1 - h] = turned

    to_band = {}
    for r in range(wins - 1, 0, -1):
        band = win + sum((1 - 2 * lax.rem(win // 2**i, 2)) * 2**i for i in range(2) if r >> i & 1)
        copy = pltpu.make_async_remote_copy(
            src_ref=chunks.at[r % 2, band],
            dst_ref=arrived.at[r],
            send_sem=win_send.at[r],
            recv_sem=win_recv.at[r],
            device_id={"win": band},
            device_id_type=MESH,
        )
        copy.start()
        to_band[r] = copy

    def piece(owner, peer, pair):
        return pltpu.make_async_remote_copy(
            src_ref=blocks.at[pair, owner],
            dst_ref=blocks.at[pair, owner],
            send_sem=pair_send.at[pair],
            recv_sem=pair_recv.at[pair, owner],
            device_id={"chan": peer},
            device_id_type=MESH,
        )

    in_first = lax.broadcasted_iota(jnp.int32, (rows, LANES), 1) < LANES // 2
    is_re = lax.broadcasted_iota(jnp.int32, (rows, LANES), 1) % (LANES // 2) < LANES // 4
    pairs = wins // 2
    left = []
    for pair in range(pairs):
        if pair > 0:
            to_band[2 * pair].wait_recv()
        to_band[2 * pair + 1].wait_recv()
        even = chunks[0, win] if pair == 0 else arrived[2 * pair]
        both = jnp.where(in_first, even.astype(jnp.int32), arrived[2 * pair + 1].astype(jnp.int32))
        blocks[pair, me] = both.astype(jnp.int16)
        for_each_peer(chans, me, lambda k, peer: piece(me, peer, pair).start())
        x = restored(both)
        right[pair, me] = jnp.concatenate(split2(x), axis=1)
        after = pltpu.roll(x, LANES - LANES // 4, 1)
        before = pltpu.roll(x, LANES // 4, 1)
        high, low = split2(jnp.concatenate([x, jnp.where(is_re, after, -before)], axis=0))
        left.append(
            jnp.concatenate(
                [
                    jnp.concatenate([high, high], axis=1),
                    jnp.concatenate([low, jnp.zeros_like(low)], axis=1),
                ],
                axis=0,
            )
        )

    scale = 1.0 / FREQ_BINS

    def term(pair, g):
        return dot_rows(left[pair], right[pair, pl.ds(g * GROUP, GROUP)].reshape(GROUP * rows, 2 * LANES))

    def finished(acc):
        return ((acc[: 2 * rows] + acc[2 * rows :]) * scale).astype(out_ref.dtype)

    def take(pair, k, peer):
        piece(peer, peer, pair).wait_recv()
        right[pair, peer] = jnp.concatenate(split2(restored(blocks[pair, peer])), axis=1)

    def take_pair(pair):
        for_each_peer(chans, me, functools.partial(take, pair), (1, 2, 3, 4, 5, 6, 7))

    if chans == GROUP:
        acc = None
        for pair in range(pairs):
            take_pair(pair)
            acc = term(pair, 0) if acc is None else acc + term(pair, 0)
        out = finished(acc)
        out_ref[0, 0] = out[:rows]
        out_ref[0, 1] = out[rows:]
    else:
        for pair in range(pairs):
            take_pair(pair)

        @pl.loop(0, chans // GROUP)
        def _(g):
            out = finished(sum(term(pair, g) for pair in range(pairs)))
            at = pl.ds(pl.multiple_of(g * (GROUP * rows), LANES), GROUP * rows)
            out_ref[0, 0, :, at] = out[:rows]
            out_ref[0, 1, :, at] = out[rows:]

    for copy in halos + list(to_band.values()):
        copy.wait_send()
    for pair in range(pairs):
        sent = blocks.at[pair, pl.ds(0, chans - 1)]
        pltpu.make_async_remote_copy(
            src_ref=sent,
            dst_ref=sent,
            send_sem=pair_send.at[pair],
            recv_sem=pair_recv.at[pair, me],
            device_id={"chan": lax.rem(me + 1, chans)},
            device_id_type=MESH,
        ).wait_send()


def body(chans, wins, strain, seg_ids, dead, radius):
    rows, windows, samples = strain.shape
    table = jnp.asarray(fourier_table(wins))
    width = 2 * FREQ_BINS
    dma = pltpu.SemaphoreType.DMA
    hbm = pl.BlockSpec(memory_space=pltpu.HBM)
    i32, i16 = jnp.int32, jnp.int16
    return pl.pallas_call(
        functools.partial(kernel, chans, wins),
        out_shape=pltpu.VMEM((1, 2, rows, chans * rows), BF16),
        in_specs=[hbm] * 5,
        out_specs=pl.BlockSpec(memory_space=pltpu.VMEM),
        scratch_shapes=[
            pltpu.VMEM((rows, samples), BF16),
            pltpu.VMEM(seg_ids.shape, i32),
            pltpu.VMEM((1, dead.shape[0]), i32),
            pltpu.VMEM((1, rows), i32),
            pltpu.VMEM(table.shape, F32),
            pltpu.VMEM((2, MOST_REACH, width), F32),
            pltpu.VMEM((2, MOST_REACH, width), F32),
            pltpu.VMEM((wins // 2, chans, rows, LANES), i16),
            pltpu.VMEM((2, wins, rows, LANES), i16),
            pltpu.VMEM((wins, rows, LANES), i16),
            pltpu.VMEM((wins // 2, chans, rows, 2 * LANES), BF16),
            dma((4,)),
            dma((TABLE_CUTS,)),
            dma((2,)),
            dma((2,)),
            dma((wins,)),
            dma((wins,)),
            dma((wins // 2,)),
            dma((wins // 2, chans)),
        ],
        compiler_params=pltpu.CompilerParams(
            collective_id=0, has_side_effects=True, vmem_limit_bytes=(63 if chans == GROUP else 48) * 2**20
        ),
    )(
        strain.reshape(rows * windows, samples),
        seg_ids,
        dead.reshape(1, -1),
        radius.reshape(1, -1),
        table,
    )


def solution(mesh):
    return jax.shard_map(
        functools.partial(body, mesh.shape["chan"], mesh.shape["win"]),
        mesh=mesh,
        in_specs=(P("chan", "win", None), P(), P(), P("chan")),
        out_specs=P("win", None, "chan", None),
        check_vma=False,
    )
```

```python
import functools
import math

import jax
import jax.numpy as jnp
import numpy as np
from jax import lax
from jax.experimental import pallas as pl
from jax.experimental.pallas import tpu as pltpu
from jax.sharding import PartitionSpec as P

SAMPLES = 1024
FREQ_BINS = 128
FIRST_BIN = 8
SMOOTH_BINS = 4
MOST_REACH = 8
FLOOR_POWER = 0.01
LANES = 128
TABLE_CUTS = 2
GROUP = 8
PEAK = 3.0
TOP_CODE = 32767.0
ROOT_SCALE = math.log2(TOP_CODE) - math.log2(PEAK) / 8.0

MESH = pl.DeviceIdType.MESH
F32 = jnp.float32
BF16 = jnp.bfloat16


def fourier_table(bands):
    band_bins = FREQ_BINS // bands
    half = SAMPLES // 2
    t = np.arange(half, dtype=np.int64)
    bins = FIRST_BIN + np.arange(FREQ_BINS, dtype=np.int64)
    angles = np.pi / SAMPLES * ((2 * t[:, None] + 1) * bins[None, :] % (2 * SAMPLES))
    taper = 0.5 - 0.5 * np.cos(2.0 * np.pi / SAMPLES * (t + 0.5))
    weights = taper[:, None] / np.sqrt(float(SAMPLES))
    cos, sin = weights * np.cos(angles), -weights * np.sin(angles)
    both = np.stack(
        [cos.reshape(half, bands, band_bins), sin.reshape(half, bands, band_bins)], axis=2
    ).reshape(half, 2 * FREQ_BINS)
    return both.astype(np.float32).reshape(TABLE_CUTS, half // TABLE_CUTS, -1)


def split3(x):
    high = x.astype(BF16)
    rest = x - high.astype(F32)
    middle = rest.astype(BF16)
    low = (rest - middle.astype(F32)).astype(BF16)
    return high, middle, low


def column_of(row, length, shift=0):
    shape = (length, row.shape[1])
    hit = lax.broadcasted_iota(jnp.int32, shape, 1) == lax.broadcasted_iota(jnp.int32, shape, 0) + shift
    return jnp.sum(jnp.where(hit, row, 0), axis=1, keepdims=True)


def links(seg, dead, radius, me, rows):
    channels, segments = seg.shape[1], dead.shape[1]
    start = me * rows - MOST_REACH
    turned = pltpu.roll(jnp.broadcast_to(seg, (8, channels)), lax.rem(channels - start, channels), 1)
    near = turned[0:1, 0:LANES]
    lane = lax.broadcasted_iota(jnp.int32, (1, LANES), 1)
    inside = (lane + start >= 0) & (lane + start < channels)
    dead_column = column_of(dead, segments)
    is_segment = lax.broadcasted_iota(jnp.int32, (segments, LANES), 0) == near
    dead_near = jnp.sum(jnp.where(is_segment, dead_column, 0), axis=0, keepdims=True)
    alive_near = jnp.where(inside, 1 - dead_near, 0)
    own_segs = column_of(near, rows, MOST_REACH)
    alive_own = column_of(alive_near, rows, MOST_REACH).astype(F32)
    reach = column_of(radius, rows)
    shape = (rows, LANES)
    offsets = lax.broadcasted_iota(jnp.int32, shape, 1) - lax.broadcasted_iota(jnp.int32, shape, 0) - MOST_REACH
    linked = (jnp.abs(offsets) <= reach) & (near == own_segs) & (alive_near > 0)
    linked = jnp.where(linked, 1.0, 0.0)
    counts = jnp.maximum(jnp.sum(linked, axis=1, keepdims=True), 1.0)
    lane = lax.broadcasted_iota(jnp.int32, shape, 1)
    own_first = pltpu.roll(linked, LANES - MOST_REACH, 1)
    linked = jnp.where(lane < rows, own_first, jnp.where(lane < rows + MOST_REACH, pltpu.roll(linked, rows, 1), linked))
    return linked[:, : rows + 2 * MOST_REACH].astype(BF16), alive_own, 1.0 / counts


def bin_of(lanes, bands):
    half = FREQ_BINS // bands
    return lanes // (2 * half) * half + lanes % half


def smoothing(bands):
    lanes = 2 * FREQ_BINS
    bins = bin_of(lax.broadcasted_iota(jnp.int32, (1, lanes), 1), bands)
    apart = bin_of(lax.broadcasted_iota(jnp.int32, (lanes, 1), 0), bands) - bins
    nearby = jnp.where(jnp.abs(apart) <= SMOOTH_BINS, 1.0, 0.0).astype(BF16)
    members = jnp.minimum(bins + SMOOTH_BINS, FREQ_BINS - 1) - jnp.maximum(bins - SMOOTH_BINS, 0) + 1
    return nearby, 1.0 / members.astype(F32)


def dot(a, b):
    return jnp.dot(a, b, preferred_element_type=F32)


def dot_rows(a, b):
    return lax.dot_general(a, b, (((1,), (1,)), ((), ())), preferred_element_type=F32)


def quantized(x, power, mean_power):
    root = jnp.exp2((jnp.log2(power) - jnp.log2(mean_power)) * 0.0625 + ROOT_SCALE)
    code = jnp.minimum(root + 0.5, TOP_CODE).astype(jnp.int32)
    return jnp.where(x < 0, -code, code)


def restored(codes):
    y = codes.astype(jnp.int32).astype(F32) * (1.0 / TOP_CODE)
    y2 = y * y
    y4 = y2 * y2
    size = (y4 * y4) * PEAK
    return jnp.where(y < 0, -size, size)


def split2(x):
    high = x.astype(BF16)
    return high, (x - high.astype(F32)).astype(BF16)


def for_each_peer(chans, me, act, order=(6, 7, 4, 5, 2, 3, 1)):
    if chans == GROUP:
        bits = [lax.rem(me // 2**i, 2) for i in range(3)]
        for k in order:
            act(k, me + sum((1 - 2 * bits[i]) * 2**i for i in range(3) if k >> i & 1))
    else:

        def step(k, carry):
            act(k, lax.rem(me + k, chans))
            return carry

        lax.fori_loop(1, chans, step, 0)


def kernel(
    chans, wins, strain_hbm, seg_hbm, dead_hbm, radius_hbm, table_hbm, out_ref,
    strain, seg, dead, radius, table, edges, halo_rows, blocks, chunks, arrived, right, load_sem, table_sem,
    halo_send, halo_recv, win_send, win_recv, pair_send, pair_recv,
):
    rows = strain_hbm.shape[0]
    width = 2 * FREQ_BINS
    me, win = lax.axis_index("chan"), lax.axis_index("win")

    strain_load = pltpu.make_async_copy(strain_hbm, strain, load_sem.at[0])
    table_loads = [
        pltpu.make_async_copy(table_hbm.at[i], table.at[i], table_sem.at[i]) for i in range(TABLE_CUTS)
    ]
    for load in [strain_load] + table_loads:
        load.start()

    barrier = pltpu.get_barrier_semaphore()

    def greet(k, peer):
        pl.semaphore_signal(barrier, inc=1, device_id={"chan": peer}, device_id_type=MESH)

    for_each_peer(chans, me, greet)
    for r in range(1, wins):
        pl.semaphore_signal(barrier, inc=1, device_id={"win": lax.rem(win + r, wins)}, device_id_type=MESH)

    loads = [
        pltpu.make_async_copy(src, dst, load_sem.at[1 + i])
        for i, (src, dst) in enumerate([(seg_hbm, seg), (dead_hbm, dead), (radius_hbm, radius)])
    ]
    for load in loads:
        load.start()

    nearby, per_member = smoothing(wins)
    for load in loads:
        load.wait()
    linked, alive, per_count = links(seg[...].reshape(1, -1), dead[...], radius[...], me, rows)

    strain_load.wait()
    cut = SAMPLES // 2 // TABLE_CUTS
    shape = (cut, cut)
    flips = lax.broadcasted_iota(jnp.int32, shape, 0) + lax.broadcasted_iota(jnp.int32, shape, 1) == cut - 1
    last_cuts = [strain[:, SAMPLES - (i + 1) * cut : SAMPLES - i * cut] for i in range(TABLE_CUTS)]
    backwards = dot(jnp.concatenate(last_cuts, axis=0), jnp.where(flips, 1.0, 0.0).astype(BF16)).astype(BF16)
    total = None
    for i in range(TABLE_CUTS):
        samples = jnp.concatenate(
            [strain[:, i * cut : (i + 1) * cut], backwards[i * rows : (i + 1) * rows]], axis=0
        )
        table_loads[i].wait()
        term = dot(samples, jnp.concatenate(split3(table[i]), axis=1))
        total = term if total is None else total + term
    total = total[:, :width] + total[:, width : 2 * width] + total[:, 2 * width :]
    is_cos = lax.broadcasted_iota(jnp.int32, (1, width), 1) % (width // wins) < width // wins // 2
    own = total[:rows] + jnp.where(is_cos, 1.0, -1.0) * total[rows:]
    edges[0] = own[rows - MOST_REACH :]
    edges[1] = own[:MOST_REACH]

    pl.semaphore_wait(barrier, chans - 1 + wins - 1)

    halos = [
        pltpu.make_async_remote_copy(
            src_ref=edges.at[side],
            dst_ref=halo_rows.at[side],
            send_sem=halo_send.at[side],
            recv_sem=halo_recv.at[side],
            device_id={"chan": lax.rem(me + step, chans)},
            device_id_type=MESH,
        )
        for side, step in enumerate((1, chans - 1))
    ]
    for halo in halos:
        halo.start()
    own_sums = dot(linked[:, :rows], jnp.concatenate(split3(own), axis=1))
    own_sums = own_sums[:, :width] + own_sums[:, width : 2 * width] + own_sums[:, 2 * width :]
    for halo in halos:
        halo.wait_recv()

    near_rows = halo_rows[...].reshape(2 * MOST_REACH, width)
    near_parts = jnp.concatenate(split3(near_rows), axis=1)
    sums = dot(linked[:, rows:], near_parts)
    sums = own_sums + (sums[:, :width] + sums[:, width : 2 * width] + sums[:, 2 * width :])
    spectra = alive * (own - sums * per_count)
    power = spectra * spectra
    smooth = dot(jnp.concatenate(split2(power), axis=0), nearby)
    smooth = (smooth[:rows] + smooth[rows:]) * per_member
    codes = quantized(spectra, power, jnp.maximum(smooth, FLOOR_POWER))

    for j in range(wins // 2):
        tile = codes[:, j * LANES : (j + 1) * LANES]
        turned = pltpu.roll(tile, LANES // 2, 1).astype(jnp.int16)
        tile = tile.astype(jnp.int16)
        for h in range(2):
            chunks[h, 2 * j + h] = tile
            chunks[h, 2 * j + 1 - h] = turned

    to_band = {}
    for r in range(wins - 1, 0, -1):
        band = win + sum((1 - 2 * lax.rem(win // 2**i, 2)) * 2**i for i in range(2) if r >> i & 1)
        copy = pltpu.make_async_remote_copy(
            src_ref=chunks.at[r % 2, band],
            dst_ref=arrived.at[r],
            send_sem=win_send.at[r],
            recv_sem=win_recv.at[r],
            device_id={"win": band},
            device_id_type=MESH,
        )
        copy.start()
        to_band[r] = copy

    def piece(owner, peer, pair):
        return pltpu.make_async_remote_copy(
            src_ref=blocks.at[pair, owner],
            dst_ref=blocks.at[pair, owner],
            send_sem=pair_send.at[pair],
            recv_sem=pair_recv.at[pair, owner],
            device_id={"chan": peer},
            device_id_type=MESH,
        )

    in_first = lax.broadcasted_iota(jnp.int32, (rows, LANES), 1) < LANES // 2
    is_re = lax.broadcasted_iota(jnp.int32, (rows, LANES), 1) % (LANES // 2) < LANES // 4
    pairs = wins // 2
    left = []
    for pair in range(pairs):
        if pair > 0:
            to_band[2 * pair].wait_recv()
        to_band[2 * pair + 1].wait_recv()
        even = chunks[0, win] if pair == 0 else arrived[2 * pair]
        both = jnp.where(in_first, even.astype(jnp.int32), arrived[2 * pair + 1].astype(jnp.int32))
        blocks[pair, me] = both.astype(jnp.int16)
        for_each_peer(chans, me, lambda k, peer: piece(me, peer, pair).start())
        x = restored(both)
        right[pair, me] = jnp.concatenate(split2(x), axis=1)
        after = pltpu.roll(x, LANES - LANES // 4, 1)
        before = pltpu.roll(x, LANES // 4, 1)
        high, low = split2(jnp.concatenate([x, jnp.where(is_re, after, -before)], axis=0))
        left.append(
            jnp.concatenate(
                [
                    jnp.concatenate([high, high], axis=1),
                    jnp.concatenate([low, jnp.zeros_like(low)], axis=1),
                ],
                axis=0,
            )
        )

    scale = 1.0 / FREQ_BINS

    def term(pair, g):
        return dot_rows(left[pair], right[pair, pl.ds(g * GROUP, GROUP)].reshape(GROUP * rows, 2 * LANES))

    def finished(acc):
        return ((acc[: 2 * rows] + acc[2 * rows :]) * scale).astype(out_ref.dtype)

    def take(pair, k, peer):
        piece(peer, peer, pair).wait_recv()
        right[pair, peer] = jnp.concatenate(split2(restored(blocks[pair, peer])), axis=1)

    def take_pair(pair):
        for_each_peer(chans, me, functools.partial(take, pair), (1, 2, 3, 4, 5, 6, 7))

    if chans == GROUP:
        acc = None
        for pair in range(pairs):
            take_pair(pair)
            acc = term(pair, 0) if acc is None else acc + term(pair, 0)
        out = finished(acc)
        out_ref[0, 0] = out[:rows]
        out_ref[0, 1] = out[rows:]
    else:
        for pair in range(pairs):
            take_pair(pair)

        @pl.loop(0, chans // GROUP)
        def _(g):
            out = finished(sum(term(pair, g) for pair in range(pairs)))
            at = pl.ds(pl.multiple_of(g * (GROUP * rows), LANES), GROUP * rows)
            out_ref[0, 0, :, at] = out[:rows]
            out_ref[0, 1, :, at] = out[rows:]

    for copy in halos + list(to_band.values()):
        copy.wait_send()
    for pair in range(pairs):
        sent = blocks.at[pair, pl.ds(0, chans - 1)]
        pltpu.make_async_remote_copy(
            src_ref=sent,
            dst_ref=sent,
            send_sem=pair_send.at[pair],
            recv_sem=pair_recv.at[pair, me],
            device_id={"chan": lax.rem(me + 1, chans)},
            device_id_type=MESH,
        ).wait_send()


def body(chans, wins, strain, seg_ids, dead, radius):
    rows, windows, samples = strain.shape
    table = jnp.asarray(fourier_table(wins))
    width = 2 * FREQ_BINS
    dma = pltpu.SemaphoreType.DMA
    hbm = pl.BlockSpec(memory_space=pltpu.HBM)
    i32, i16 = jnp.int32, jnp.int16
    return pl.pallas_call(
        functools.partial(kernel, chans, wins),
        out_shape=pltpu.VMEM((1, 2, rows, chans * rows), BF16),
        in_specs=[hbm] * 5,
        out_specs=pl.BlockSpec(memory_space=pltpu.VMEM),
        scratch_shapes=[
            pltpu.VMEM((rows, samples), BF16),
            pltpu.VMEM(seg_ids.shape, i32),
            pltpu.VMEM((1, dead.shape[0]), i32),
            pltpu.VMEM((1, rows), i32),
            pltpu.VMEM(table.shape, F32),
            pltpu.VMEM((2, MOST_REACH, width), F32),
            pltpu.VMEM((2, MOST_REACH, width), F32),
            pltpu.VMEM((wins // 2, chans, rows, LANES), i16),
            pltpu.VMEM((2, wins, rows, LANES), i16),
            pltpu.VMEM((wins, rows, LANES), i16),
            pltpu.VMEM((wins // 2, chans, rows, 2 * LANES), BF16),
            dma((4,)),
            dma((TABLE_CUTS,)),
            dma((2,)),
            dma((2,)),
            dma((wins,)),
            dma((wins,)),
            dma((wins // 2,)),
            dma((wins // 2, chans)),
        ],
        compiler_params=pltpu.CompilerParams(
            collective_id=0, has_side_effects=True, vmem_limit_bytes=(63 if chans == GROUP else 48) * 2**20
        ),
    )(
        strain.reshape(rows * windows, samples),
        seg_ids,
        dead.reshape(1, -1),
        radius.reshape(1, -1),
        table,
    )


def solution(mesh):
    return jax.shard_map(
        functools.partial(body, mesh.shape["chan"], mesh.shape["win"]),
        mesh=mesh,
        in_specs=(P("chan", "win", None), P(), P(), P("chan")),
        out_specs=P("win", None, "chan", None),
        check_vma=False,
    )
```

```python
import functools
import math

import jax
import jax.numpy as jnp
import numpy as np
from jax import lax
from jax.experimental import pallas as pl
from jax.experimental.pallas import tpu as pltpu
from jax.sharding import PartitionSpec as P

SAMPLES = 1024
FREQ_BINS = 128
FIRST_BIN = 8
SMOOTH_BINS = 4
MOST_REACH = 8
FLOOR_POWER = 0.01
LANES = 128
TABLE_CUTS = 2
GROUP = 8
PEAK = 3.0
TOP_CODE = 32767.0
ROOT_SCALE = math.log2(TOP_CODE) - math.log2(PEAK) / 8.0

MESH = pl.DeviceIdType.MESH
F32 = jnp.float32
BF16 = jnp.bfloat16


def fourier_table(bands):
    band_bins = FREQ_BINS // bands
    half = SAMPLES // 2
    t = np.arange(half, dtype=np.int64)
    bins = FIRST_BIN + np.arange(FREQ_BINS, dtype=np.int64)
    angles = np.pi / SAMPLES * ((2 * t[:, None] + 1) * bins[None, :] % (2 * SAMPLES))
    taper = 0.5 - 0.5 * np.cos(2.0 * np.pi / SAMPLES * (t + 0.5))
    weights = taper[:, None] / np.sqrt(float(SAMPLES))
    cos, sin = weights * np.cos(angles), -weights * np.sin(angles)
    both = np.stack(
        [cos.reshape(half, bands, band_bins), sin.reshape(half, bands, band_bins)], axis=2
    ).reshape(half, 2 * FREQ_BINS)
    return both.astype(np.float32).reshape(TABLE_CUTS, half // TABLE_CUTS, -1)


def split3(x):
    high = x.astype(BF16)
    rest = x - high.astype(F32)
    middle = rest.astype(BF16)
    low = (rest - middle.astype(F32)).astype(BF16)
    return high, middle, low


def column_of(row, length, shift=0):
    shape = (length, row.shape[1])
    hit = lax.broadcasted_iota(jnp.int32, shape, 1) == lax.broadcasted_iota(jnp.int32, shape, 0) + shift
    return jnp.sum(jnp.where(hit, row, 0), axis=1, keepdims=True)


def links(seg, dead, radius, me, rows):
    channels, segments = seg.shape[1], dead.shape[1]
    start = me * rows - MOST_REACH
    turned = pltpu.roll(jnp.broadcast_to(seg, (8, channels)), lax.rem(channels - start, channels), 1)
    near = turned[0:1, 0:LANES]
    lane = lax.broadcasted_iota(jnp.int32, (1, LANES), 1)
    inside = (lane + start >= 0) & (lane + start < channels)
    dead_column = column_of(dead, segments)
    is_segment = lax.broadcasted_iota(jnp.int32, (segments, LANES), 0) == near
    dead_near = jnp.sum(jnp.where(is_segment, dead_column, 0), axis=0, keepdims=True)
    alive_near = jnp.where(inside, 1 - dead_near, 0)
    own_segs = column_of(near, rows, MOST_REACH)
    alive_own = column_of(alive_near, rows, MOST_REACH).astype(F32)
    reach = column_of(radius, rows)
    shape = (rows, LANES)
    offsets = lax.broadcasted_iota(jnp.int32, shape, 1) - lax.broadcasted_iota(jnp.int32, shape, 0) - MOST_REACH
    linked = (jnp.abs(offsets) <= reach) & (near == own_segs) & (alive_near > 0)
    linked = jnp.where(linked, 1.0, 0.0)
    counts = jnp.maximum(jnp.sum(linked, axis=1, keepdims=True), 1.0)
    lane = lax.broadcasted_iota(jnp.int32, shape, 1)
    own_first = pltpu.roll(linked, LANES - MOST_REACH, 1)
    linked = jnp.where(lane < rows, own_first, jnp.where(lane < rows + MOST_REACH, pltpu.roll(linked, rows, 1), linked))
    return linked[:, : rows + 2 * MOST_REACH].astype(BF16), alive_own, 1.0 / counts


def bin_of(lanes, bands):
    half = FREQ_BINS // bands
    return lanes // (2 * half) * half + lanes % half


def smoothing(bands):
    lanes = 2 * FREQ_BINS
    bins = bin_of(lax.broadcasted_iota(jnp.int32, (1, lanes), 1), bands)
    apart = bin_of(lax.broadcasted_iota(jnp.int32, (lanes, 1), 0), bands) - bins
    nearby = jnp.where(jnp.abs(apart) <= SMOOTH_BINS, 1.0, 0.0).astype(BF16)
    members = jnp.minimum(bins + SMOOTH_BINS, FREQ_BINS - 1) - jnp.maximum(bins - SMOOTH_BINS, 0) + 1
    return nearby, 1.0 / members.astype(F32)


def dot(a, b):
    return jnp.dot(a, b, preferred_element_type=F32)


def dot_rows(a, b):
    return lax.dot_general(a, b, (((1,), (1,)), ((), ())), preferred_element_type=F32)


def quantized(x, power, mean_power):
    root = jnp.exp2((jnp.log2(power) - jnp.log2(mean_power)) * 0.0625 + ROOT_SCALE)
    code = jnp.minimum(root + 0.5, TOP_CODE).astype(jnp.int32)
    return jnp.where(x < 0, -code, code)


def restored(codes):
    y = codes.astype(jnp.int32).astype(F32) * (1.0 / TOP_CODE)
    y2 = y * y
    y4 = y2 * y2
    size = (y4 * y4) * PEAK
    return jnp.where(y < 0, -size, size)


def split2(x):
    high = x.astype(BF16)
    return high, (x - high.astype(F32)).astype(BF16)


def for_each_peer(chans, me, act, order=(6, 7, 4, 5, 2, 3, 1)):
    if chans == GROUP:
        bits = [lax.rem(me // 2**i, 2) for i in range(3)]
        for k in order:
            act(k, me + sum((1 - 2 * bits[i]) * 2**i for i in range(3) if k >> i & 1))
    else:

        def step(k, carry):
            act(k, lax.rem(me + k, chans))
            return carry

        lax.fori_loop(1, chans, step, 0)


def kernel(
    chans, wins, strain_hbm, seg_hbm, dead_hbm, radius_hbm, table_hbm, out_ref,
    strain, seg, dead, radius, table, edges, halo_rows, blocks, chunks, arrived, right, load_sem, table_sem,
    halo_send, halo_recv, win_send, win_recv, pair_send, pair_recv,
):
    rows = strain_hbm.shape[0]
    width = 2 * FREQ_BINS
    me, win = lax.axis_index("chan"), lax.axis_index("win")

    strain_load = pltpu.make_async_copy(strain_hbm, strain, load_sem.at[0])
    table_loads = [
        pltpu.make_async_copy(table_hbm.at[i], table.at[i], table_sem.at[i]) for i in range(TABLE_CUTS)
    ]
    for load in [strain_load] + table_loads:
        load.start()

    barrier = pltpu.get_barrier_semaphore()

    def greet(k, peer):
        pl.semaphore_signal(barrier, inc=1, device_id={"chan": peer}, device_id_type=MESH)

    for_each_peer(chans, me, greet)
    for r in range(1, wins):
        pl.semaphore_signal(barrier, inc=1, device_id={"win": lax.rem(win + r, wins)}, device_id_type=MESH)

    loads = [
        pltpu.make_async_copy(src, dst, load_sem.at[1 + i])
        for i, (src, dst) in enumerate([(seg_hbm, seg), (dead_hbm, dead), (radius_hbm, radius)])
    ]
    for load in loads:
        load.start()

    nearby, per_member = smoothing(wins)
    for load in loads:
        load.wait()
    linked, alive, per_count = links(seg[...].reshape(1, -1), dead[...], radius[...], me, rows)

    strain_load.wait()
    cut = SAMPLES // 2 // TABLE_CUTS
    shape = (cut, cut)
    flips = lax.broadcasted_iota(jnp.int32, shape, 0) + lax.broadcasted_iota(jnp.int32, shape, 1) == cut - 1
    last_cuts = [strain[:, SAMPLES - (i + 1) * cut : SAMPLES - i * cut] for i in range(TABLE_CUTS)]
    backwards = dot(jnp.concatenate(last_cuts, axis=0), jnp.where(flips, 1.0, 0.0).astype(BF16)).astype(BF16)
    total = None
    for i in range(TABLE_CUTS):
        samples = jnp.concatenate(
            [strain[:, i * cut : (i + 1) * cut], backwards[i * rows : (i + 1) * rows]], axis=0
        )
        table_loads[i].wait()
        term = dot(samples, jnp.concatenate(split3(table[i]), axis=1))
        total = term if total is None else total + term
    total = total[:, :width] + total[:, width : 2 * width] + total[:, 2 * width :]
    is_cos = lax.broadcasted_iota(jnp.int32, (1, width), 1) % (width // wins) < width // wins // 2
    own = total[:rows] + jnp.where(is_cos, 1.0, -1.0) * total[rows:]
    edges[0] = own[rows - MOST_REACH :]
    edges[1] = own[:MOST_REACH]

    pl.semaphore_wait(barrier, chans - 1 + wins - 1)

    halos = [
        pltpu.make_async_remote_copy(
            src_ref=edges.at[side],
            dst_ref=halo_rows.at[side],
            send_sem=halo_send.at[side],
            recv_sem=halo_recv.at[side],
            device_id={"chan": lax.rem(me + step, chans)},
            device_id_type=MESH,
        )
        for side, step in enumerate((1, chans - 1))
    ]
    for halo in halos:
        halo.start()
    own_sums = dot(linked[:, :rows], jnp.concatenate(split3(own), axis=1))
    own_sums = own_sums[:, :width] + own_sums[:, width : 2 * width] + own_sums[:, 2 * width :]
    for halo in halos:
        halo.wait_recv()

    near_rows = halo_rows[...].reshape(2 * MOST_REACH, width)
    near_parts = jnp.concatenate(split3(near_rows), axis=1)
    sums = dot(linked[:, rows:], near_parts)
    sums = own_sums + (sums[:, :width] + sums[:, width : 2 * width] + sums[:, 2 * width :])
    spectra = alive * (own - sums * per_count)
    power = spectra * spectra
    smooth = dot(jnp.concatenate(split2(power), axis=0), nearby)
    smooth = (smooth[:rows] + smooth[rows:]) * per_member
    codes = quantized(spectra, power, jnp.maximum(smooth, FLOOR_POWER))

    for j in range(wins // 2):
        tile = codes[:, j * LANES : (j + 1) * LANES]
        turned = pltpu.roll(tile, LANES // 2, 1).astype(jnp.int16)
        tile = tile.astype(jnp.int16)
        for h in range(2):
            chunks[h, 2 * j + h] = tile
            chunks[h, 2 * j + 1 - h] = turned

    to_band = {}
    for r in range(wins - 1, 0, -1):
        band = win + sum((1 - 2 * lax.rem(win // 2**i, 2)) * 2**i for i in range(2) if r >> i & 1)
        copy = pltpu.make_async_remote_copy(
            src_ref=chunks.at[r % 2, band],
            dst_ref=arrived.at[r],
            send_sem=win_send.at[r],
            recv_sem=win_recv.at[r],
            device_id={"win": band},
            device_id_type=MESH,
        )
        copy.start()
        to_band[r] = copy

    def piece(owner, peer, pair):
        return pltpu.make_async_remote_copy(
            src_ref=blocks.at[pair, owner],
            dst_ref=blocks.at[pair, owner],
            send_sem=pair_send.at[pair],
            recv_sem=pair_recv.at[pair, owner],
            device_id={"chan": peer},
            device_id_type=MESH,
        )

    in_first = lax.broadcasted_iota(jnp.int32, (rows, LANES), 1) < LANES // 2
    is_re = lax.broadcasted_iota(jnp.int32, (rows, LANES), 1) % (LANES // 2) < LANES // 4
    pairs = wins // 2
    left = []
    for pair in range(pairs):
        if pair > 0:
            to_band[2 * pair].wait_recv()
        to_band[2 * pair + 1].wait_recv()
        even = chunks[0, win] if pair == 0 else arrived[2 * pair]
        both = jnp.where(in_first, even.astype(jnp.int32), arrived[2 * pair + 1].astype(jnp.int32))
        blocks[pair, me] = both.astype(jnp.int16)
        for_each_peer(chans, me, lambda k, peer: piece(me, peer, pair).start())
        x = restored(both)
        right[pair, me] = jnp.concatenate(split2(x), axis=1)
        after = pltpu.roll(x, LANES - LANES // 4, 1)
        before = pltpu.roll(x, LANES // 4, 1)
        high, low = split2(jnp.concatenate([x, jnp.where(is_re, after, -before)], axis=0))
        left.append(jnp.concatenate([high, high, low], axis=1))

    scale = 1.0 / FREQ_BINS

    def term(pair, g):
        parts = right[pair, pl.ds(g * GROUP, GROUP)].reshape(GROUP * rows, 2 * LANES)
        return dot_rows(left[pair], jnp.concatenate([parts, parts[:, :LANES]], axis=1))

    def finished(acc):
        return (acc * scale).astype(out_ref.dtype)

    def take(pair, k, peer):
        piece(peer, peer, pair).wait_recv()
        right[pair, peer] = jnp.concatenate(split2(restored(blocks[pair, peer])), axis=1)

    def take_pair(pair):
        for_each_peer(chans, me, functools.partial(take, pair), (1, 2, 3, 4, 5, 6, 7))

    if chans == GROUP:
        acc = None
        for pair in range(pairs):
            take_pair(pair)
            acc = term(pair, 0) if acc is None else acc + term(pair, 0)
        out = finished(acc)
        out_ref[0, 0] = out[:rows]
        out_ref[0, 1] = out[rows:]
    else:
        for pair in range(pairs):
            take_pair(pair)

        @pl.loop(0, chans // GROUP)
        def _(g):
            out = finished(sum(term(pair, g) for pair in range(pairs)))
            at = pl.ds(pl.multiple_of(g * (GROUP * rows), LANES), GROUP * rows)
            out_ref[0, 0, :, at] = out[:rows]
            out_ref[0, 1, :, at] = out[rows:]

    for copy in halos + list(to_band.values()):
        copy.wait_send()
    for pair in range(pairs):
        sent = blocks.at[pair, pl.ds(0, chans - 1)]
        pltpu.make_async_remote_copy(
            src_ref=sent,
            dst_ref=sent,
            send_sem=pair_send.at[pair],
            recv_sem=pair_recv.at[pair, me],
            device_id={"chan": lax.rem(me + 1, chans)},
            device_id_type=MESH,
        ).wait_send()


def body(chans, wins, strain, seg_ids, dead, radius):
    rows, windows, samples = strain.shape
    table = jnp.asarray(fourier_table(wins))
    width = 2 * FREQ_BINS
    dma = pltpu.SemaphoreType.DMA
    hbm = pl.BlockSpec(memory_space=pltpu.HBM)
    i32, i16 = jnp.int32, jnp.int16
    return pl.pallas_call(
        functools.partial(kernel, chans, wins),
        out_shape=pltpu.VMEM((1, 2, rows, chans * rows), BF16),
        in_specs=[hbm] * 5,
        out_specs=pl.BlockSpec(memory_space=pltpu.VMEM),
        scratch_shapes=[
            pltpu.VMEM((rows, samples), BF16),
            pltpu.VMEM(seg_ids.shape, i32),
            pltpu.VMEM((1, dead.shape[0]), i32),
            pltpu.VMEM((1, rows), i32),
            pltpu.VMEM(table.shape, F32),
            pltpu.VMEM((2, MOST_REACH, width), F32),
            pltpu.VMEM((2, MOST_REACH, width), F32),
            pltpu.VMEM((wins // 2, chans, rows, LANES), i16),
            pltpu.VMEM((2, wins, rows, LANES), i16),
            pltpu.VMEM((wins, rows, LANES), i16),
            pltpu.VMEM((wins // 2, chans, rows, 2 * LANES), BF16),
            dma((4,)),
            dma((TABLE_CUTS,)),
            dma((2,)),
            dma((2,)),
            dma((wins,)),
            dma((wins,)),
            dma((wins // 2,)),
            dma((wins // 2, chans)),
        ],
        compiler_params=pltpu.CompilerParams(
            collective_id=0, has_side_effects=True, vmem_limit_bytes=(63 if chans == GROUP else 48) * 2**20
        ),
    )(
        strain.reshape(rows * windows, samples),
        seg_ids,
        dead.reshape(1, -1),
        radius.reshape(1, -1),
        table,
    )


def solution(mesh):
    return jax.shard_map(
        functools.partial(body, mesh.shape["chan"], mesh.shape["win"]),
        mesh=mesh,
        in_specs=(P("chan", "win", None), P(), P(), P("chan")),
        out_specs=P("win", None, "chan", None),
        check_vma=False,
    )
```
